32 devices in a mesh: seq: 4 (over y, x), ctx: 2 (over core), head: 4 (over z).
Axes of the slice: x: 2, y: 2, z: 4, core: 2. Of those that a mesh axis runs over, the one named last changes fastest.
Arguments:
- queries: bfloat16 [4, 2, 512, 2048], P('seq', None, 'ctx', 'head'), may hold values from -8 to 8
- key_vectors: bfloat16 [4, 2, 512, 2048], P('seq', None, 'ctx', 'head'), may hold values from -8 to 8
- value_vectors: bfloat16 [4, 2, 512, 2048], P('seq', None, 'ctx', 'head'), may hold values from -6 to 6
- token_rates: float32 [4, 2, 512, 8], P('seq', None, 'ctx', 'head'), may hold values from 0.003 to 0.03
- fast_in: bfloat16 [8, 256, 512], P('head'), may hold values from -0.375 to 0.375
- fast_gate: bfloat16 [8, 256, 512], P('head'), may hold values from -0.375 to 0.375
- fast_out: bfloat16 [8, 512, 256], P('head'), may hold values from -0.25 to 0.25
- out_gain: float32 [2048], P('head'), may hold values from 0.1 to 1.9
- out_weight: bfloat16 [2048, 2048], P('head'), may hold values from -0.125 to 0.125
- cotangent: bfloat16 [4, 2, 512, 2048], P('seq', None, 'ctx', 'head'), may hold values from -6 to 6
Outputs:
- layer_out: bfloat16 [4, 2, 512, 2048], P('seq', None, 'ctx', 'head')
- weight_grad: float32 [2048, 2048], P('head', ('seq', 'ctx'))
- final_in: float32 [4, 8, 256, 512], P('seq', 'head')
- final_gate: float32 [4, 8, 256, 512], P('seq', 'head')
- final_out: float32 [4, 8, 512, 256], P('seq', 'head')
The draws below stay inside these ranges and needn't reach their ends.
All inputs are finite; a program needn't handle non-finite values.
Results may differ from the reference program's by a relative error of at most 0.024.
Values may be sent and summed in bfloat16 or wider, within the bound.
A program may use at most 128 MiB of HBM per device.

```python
import math
import jax
import jax.numpy as jnp
from jax import lax

DH = 256
FH = 512
NCH = 2
SEQS = 4
GROUP = 512
WIN = 256
HEADS = 8
D = 2048


def drawn_pair(key):
    full_shape = (SEQS, NCH, GROUP, D)
    drawn_query = jnp.clip(jax.random.normal(jax.random.fold_in(key, 101), full_shape, jnp.float32), -6.0, 6.0)
    drawn_keys = jnp.clip(jax.random.normal(jax.random.fold_in(key, 102), full_shape, jnp.float32), -6.0, 6.0)
    return (drawn_query, drawn_keys)


def draw_queries(key, part):
    return drawn_pair(key)[0].astype(jnp.bfloat16)


def draw_key_vectors(key, part):
    return drawn_pair(key)[1].astype(jnp.bfloat16)


def with_spikes(result, stream_key, source, target, parts, factor):
    owner, partner = [(jnp.arange(result.shape[axis_at]) // (result.shape[axis_at] // parts)).reshape([-1 if axis == axis_at else 1 for axis in range(result.ndim)]) for axis_at in (source, target)]
    chosen = jax.random.permutation(stream_key, parts)[partner]
    strong = (owner == chosen) | (owner == (partner + parts // 2) % parts)
    return jnp.where(strong, factor * result, result)


def levels(rng, shape, shards, least, high):
    gain = 1.0
    for axis_at, blocks in shards:
        heights = jax.random.uniform(jax.random.fold_in(jax.random.fold_in(rng, 6), axis_at), (blocks,), jnp.float32, least / len(shards), high / len(shards))
        gain = gain * jnp.repeat(jnp.exp(heights), shape[axis_at] // blocks).reshape((-1,) + (1,) * (len(shape) - 1 - axis_at))
    return gain


def normal_values(key, dims, width, reach, split=(), kind=jnp.bfloat16):
    array = jax.random.normal(key, dims, jnp.float32) * width
    if len(split) > 0:
        array = levels(key, dims, split, -0.22, 0.18) * array
    return jnp.clip(array, min=-reach, max=reach).astype(kind)


def noise_with(stream_key, dims, spread, limit, cuts, heavy, kind=jnp.bfloat16):
    values = spread * jax.random.normal(stream_key, dims, jnp.float32)
    if cuts:
        values = values * levels(stream_key, dims, cuts, -0.22, 0.18)
    return jnp.clip(with_spikes(values, jax.random.fold_in(stream_key, 3), *heavy), -limit, limit).astype(kind)


def setup_inputs(seed: int = 0) -> dict:
    key_list = jax.random.split(jax.random.key(seed), 11)
    return {
        "queries": draw_queries(jax.random.fold_in(key_list[10], 71), 0),
        "key_vectors": draw_key_vectors(jax.random.fold_in(key_list[10], 71), 0),
        "value_vectors": normal_values(key_list[2], (SEQS, NCH, GROUP, D), 1.0, 6.0, ((0, 4), (2, 2), (3, 4))),
        "token_rates": jnp.clip(jnp.exp(math.log(0.03) - 2.3025851 * jax.random.uniform(key_list[3], (SEQS, NCH, GROUP, HEADS), jnp.float32) ** levels(key_list[3], (SEQS, NCH, GROUP, HEADS), ((0, 4), (2, 2), (3, 4)), -0.2, 0.2)), 0.003, 0.03),
        "fast_in": normal_values(key_list[4], (HEADS, DH, FH), DH ** -0.5, 0.375, ((0, 4),)),
        "fast_gate": normal_values(key_list[5], (HEADS, DH, FH), DH ** -0.5, 0.375, ((0, 4),)),
        "fast_out": normal_values(key_list[6], (HEADS, FH, DH), FH ** -0.5, 0.25, ((0, 4),)),
        "out_gain": jnp.clip(1.0 + 0.18 * jax.random.normal(key_list[7], (D,), jnp.float32), 0.1, 1.9),
        "out_weight": normal_values(key_list[8], (D, D), D ** -0.5, 0.125, ((0, 4),)),
        "cotangent": noise_with(key_list[9], (SEQS, NCH, GROUP, D), 1.0, 6.0, ((0, 4), (2, 2), (3, 4)), (2, 3, 4, 2.0)),
    }


def normalize_rms(values_in, epsilon):
    return values_in * lax.rsqrt(lax.optimization_barrier(jnp.mean(values_in * values_in, axis=-1, keepdims=True)) + epsilon)

def column_norms(weight):
    return jnp.sqrt(lax.optimization_barrier(jnp.sum(weight * weight, axis=-2, keepdims=True)) + 1e-06)

def renorm(weight, target):
    return weight * (target / jnp.sqrt(lax.optimization_barrier(jnp.sum(weight * weight, axis=-2, keepdims=True)) + 1e-06))

def fast_head(head_in, head_gate, head_out, query_head, key_head, value_head, rate_head):
    weight_in = head_in.astype(jnp.float32)
    weight_gate = head_gate.astype(jnp.float32)
    weight_out = head_out.astype(jnp.float32)
    target_in = column_norms(weight_in)
    target_gate = column_norms(weight_gate)
    target_out = column_norms(weight_out)
    results = []
    for block_index in range(NCH):
        query_norm = normalize_rms(query_head[block_index].astype(jnp.float32), 1e-05).astype(jnp.bfloat16)
        key_norm = normalize_rms(key_head[block_index].astype(jnp.float32), 1e-05).astype(jnp.bfloat16)
        round_in = weight_in.astype(jnp.bfloat16)
        round_gate = weight_gate.astype(jnp.bfloat16)
        round_out = weight_out.astype(jnp.bfloat16)
        hidden = (jax.nn.silu(jnp.dot(query_norm, round_in, preferred_element_type=jnp.float32)) * jnp.dot(query_norm, round_gate, preferred_element_type=jnp.float32)).astype(jnp.bfloat16)
        results.append(jnp.dot(hidden, round_out, preferred_element_type=jnp.float32))
        key_in = jnp.dot(key_norm, round_in, preferred_element_type=jnp.float32)
        key_gate = jnp.dot(key_norm, round_gate, preferred_element_type=jnp.float32)
        sigmoid_in = jax.nn.sigmoid(key_in)
        active = key_in * sigmoid_in
        feature = (active * key_gate).astype(jnp.bfloat16)
        scaled_values = (rate_head[block_index][:, None] * value_head[block_index].astype(jnp.float32)).astype(jnp.bfloat16)
        d_feature = jnp.dot(scaled_values, round_out.T, preferred_element_type=jnp.float32)
        d_in = (d_feature * key_gate * sigmoid_in * (1.0 + key_in * (1.0 - sigmoid_in))).astype(jnp.bfloat16)
        d_gate = (d_feature * active).astype(jnp.bfloat16)
        weight_in = renorm(weight_in + jnp.dot(key_norm.T, d_in, preferred_element_type=jnp.float32), target_in)
        weight_gate = renorm(weight_gate + jnp.dot(key_norm.T, d_gate, preferred_element_type=jnp.float32), target_gate)
        weight_out = renorm(weight_out + jnp.dot(feature.T, scaled_values, preferred_element_type=jnp.float32), target_out)
    return (jnp.stack(results), weight_in, weight_gate, weight_out)

def window_attention(query_seq, key_seq, value_seq):
    length = query_seq.shape[0]
    blocks = length // WIN
    padded_keys = jnp.concatenate([jnp.zeros((WIN,) + key_seq.shape[1:], key_seq.dtype), key_seq], axis=0)
    padded_values = jnp.concatenate([jnp.zeros((WIN,) + value_seq.shape[1:], value_seq.dtype), value_seq], axis=0)
    score_scale = 1.0 / math.sqrt(DH)
    query_pos = jnp.arange(WIN, dtype=jnp.int32)[:, None]
    key_pos = jnp.arange(2 * WIN, dtype=jnp.int32)[None, :]

    def attend_block(block_number):
        start_row = (block_number * WIN).astype(jnp.int32)
        query_block = lax.dynamic_slice_in_dim(query_seq, start_row, WIN, 0).astype(jnp.float32)
        key_block = lax.dynamic_slice_in_dim(padded_keys, start_row, 2 * WIN, 0).astype(jnp.float32)
        value_block = lax.dynamic_slice_in_dim(padded_values, start_row, 2 * WIN, 0).astype(jnp.float32)
        scores = jnp.einsum('qhd,khd->hqk', query_block, key_block) * score_scale
        allowed = (key_pos > query_pos) & (key_pos <= query_pos + WIN) & (start_row + key_pos >= WIN)
        scores = jnp.where(allowed[None], scores, -jnp.inf)
        largest = lax.optimization_barrier(jnp.max(scores, axis=-1, keepdims=True))
        powers = jnp.exp(scores - largest)
        attn_weights = (powers / lax.optimization_barrier(jnp.sum(powers, axis=-1, keepdims=True))).astype(jnp.bfloat16)
        return jnp.einsum('hqk,khd->qhd', attn_weights.astype(jnp.float32), value_block)
    results = lax.map(attend_block, jnp.arange(blocks, dtype=jnp.int32))
    return results.reshape(length, HEADS, DH)

def reference(queries, key_vectors, value_vectors, token_rates, fast_in, fast_gate, fast_out, out_gain, out_weight, cotangent):
    length = NCH * GROUP
    mixed_list = []
    final_ins = []
    final_gates = []
    final_outs = []
    grad_total = jnp.zeros((D, D), jnp.float32)
    for sequence in range(SEQS):
        query_heads = jnp.moveaxis(queries[sequence].reshape(NCH, GROUP, HEADS, DH), 2, 0)
        key_heads = jnp.moveaxis(key_vectors[sequence].reshape(NCH, GROUP, HEADS, DH), 2, 0)
        value_heads = jnp.moveaxis(value_vectors[sequence].reshape(NCH, GROUP, HEADS, DH), 2, 0)
        rate_heads = jnp.moveaxis(token_rates[sequence], 2, 0)
        fast_result, final_one, final_two, final_three = lax.map(lambda packed: fast_head(*packed), (fast_in, fast_gate, fast_out, query_heads, key_heads, value_heads, rate_heads))
        fast_flat = jnp.moveaxis(fast_result, 0, 2).reshape(length, HEADS, DH)
        attended = window_attention(queries[sequence].reshape(length, HEADS, DH), key_vectors[sequence].reshape(length, HEADS, DH), value_vectors[sequence].reshape(length, HEADS, DH))
        combined = (normalize_rms(fast_flat, 1e-05) * out_gain.reshape(HEADS, DH) + attended).astype(jnp.bfloat16).reshape(length, D)
        mixed_list.append(jnp.dot(combined, out_weight, preferred_element_type=jnp.float32).astype(jnp.bfloat16).reshape(NCH, GROUP, D))
        grad_total = grad_total + jnp.dot(combined.T, cotangent[sequence].reshape(length, D), preferred_element_type=jnp.float32)
        final_ins.append(final_one)
        final_gates.append(final_two)
        final_outs.append(final_three)
    return (jnp.stack(mixed_list), grad_total, jnp.stack(final_ins), jnp.stack(final_gates), jnp.stack(final_outs))
```

```python
import functools
import math

import jax
import jax.numpy as jnp
from jax import lax
from jax.experimental import pallas as pl
from jax.experimental.pallas import tpu as pltpu
from jax.sharding import PartitionSpec as P


def passed_along(value, axis, steps):
    count = lax.axis_size(axis)
    pairs = [(source, (source + steps) % count) for source in range(count)]
    return lax.ppermute(value, axis, pairs)


def normalize_rms(values_in, epsilon):
    return values_in * lax.rsqrt(jnp.mean(values_in * values_in, axis=-1, keepdims=True) + epsilon)


def column_norms(weight):
    return jnp.sqrt(jnp.sum(weight * weight, axis=-2, keepdims=True) + 1e-06)


def renorm(weight, target):
    return weight * (target / jnp.sqrt(jnp.sum(weight * weight, axis=-2, keepdims=True) + 1e-06))


def shards(
    queries,
    key_vectors,
    value_vectors,
    token_rates,
    fast_in,
    fast_gate,
    fast_out,
    out_gain,
    out_weight,
    cotangent,
):
    local_heads, head_width, hidden_width = fast_in.shape
    block_count = queries.shape[1]
    row_count = queries.shape[2]
    ctx_index = lax.axis_index("ctx")
    query_rows = queries[0].reshape(block_count, row_count, local_heads, head_width)
    key_rows = key_vectors[0].reshape(block_count, row_count, local_heads, head_width)
    value_rows = value_vectors[0].reshape(block_count, row_count, local_heads, head_width)
    weight_in = fast_in.astype(jnp.float32)
    weight_gate = fast_gate.astype(jnp.float32)
    weight_out = fast_out.astype(jnp.float32)
    target_in = column_norms(weight_in)
    target_gate = column_norms(weight_gate)
    target_out = column_norms(weight_out)
    fast_outputs = []
    for block_index in range(block_count):
        query_norm = normalize_rms(query_rows[block_index].astype(jnp.float32), 1e-05).astype(
            jnp.bfloat16
        )
        key_norm = normalize_rms(key_rows[block_index].astype(jnp.float32), 1e-05).astype(
            jnp.bfloat16
        )
        round_in = weight_in.astype(jnp.bfloat16)
        round_gate = weight_gate.astype(jnp.bfloat16)
        round_out = weight_out.astype(jnp.bfloat16)
        hidden = (
            jax.nn.silu(
                jnp.einsum("thd,hdf->thf", query_norm, round_in, preferred_element_type=jnp.float32)
            )
            * jnp.einsum("thd,hdf->thf", query_norm, round_gate, preferred_element_type=jnp.float32)
        ).astype(jnp.bfloat16)
        fast_outputs.append(
            jnp.einsum("thf,hfd->thd", hidden, round_out, preferred_element_type=jnp.float32)
        )
        key_in = jnp.einsum("thd,hdf->thf", key_norm, round_in, preferred_element_type=jnp.float32)
        key_gate = jnp.einsum(
            "thd,hdf->thf", key_norm, round_gate, preferred_element_type=jnp.float32
        )
        sigmoid_in = jax.nn.sigmoid(key_in)
        active = key_in * sigmoid_in
        feature = (active * key_gate).astype(jnp.bfloat16)
        scaled_values = (
            token_rates[0, block_index][:, :, None] * value_rows[block_index].astype(jnp.float32)
        ).astype(jnp.bfloat16)
        d_feature = jnp.einsum(
            "thd,hfd->thf", scaled_values, round_out, preferred_element_type=jnp.float32
        )
        d_in = (d_feature * key_gate * sigmoid_in * (1.0 + key_in * (1.0 - sigmoid_in))).astype(
            jnp.bfloat16
        )
        d_gate = (d_feature * active).astype(jnp.bfloat16)
        update_in = jnp.einsum("thd,thf->hdf", key_norm, d_in, preferred_element_type=jnp.float32)
        update_gate = jnp.einsum(
            "thd,thf->hdf", key_norm, d_gate, preferred_element_type=jnp.float32
        )
        update_out = jnp.einsum(
            "thf,thd->hfd", feature, scaled_values, preferred_element_type=jnp.float32
        )
        total_in, total_gate, total_out = lax.psum((update_in, update_gate, update_out), "ctx")
        weight_in = renorm(weight_in + total_in, target_in)
        weight_gate = renorm(weight_gate + total_gate, target_gate)
        weight_out = renorm(weight_out + total_out, target_out)
    rim_keys, rim_values = passed_along((key_vectors[0], value_vectors[0]), "ctx", 1)
    earlier_keys = jnp.concatenate([jnp.zeros_like(rim_keys[:1]), rim_keys[:-1]], axis=0)
    earlier_values = jnp.concatenate([jnp.zeros_like(rim_values[:1]), rim_values[:-1]], axis=0)
    is_first = ctx_index == 0
    rim_keys = jnp.where(is_first, earlier_keys, rim_keys)
    rim_values = jnp.where(is_first, earlier_values, rim_values)
    window_keys = jnp.concatenate([rim_keys, key_vectors[0]], axis=1).reshape(
        block_count, 2 * row_count, local_heads, head_width
    )
    window_values = jnp.concatenate([rim_values, value_vectors[0]], axis=1).reshape(
        block_count, 2 * row_count, local_heads, head_width
    )
    scores = jnp.einsum(
        "cqhd,ckhd->chqk", query_rows, window_keys, preferred_element_type=jnp.float32
    ) * (1.0 / math.sqrt(head_width))
    query_pos = jnp.arange(row_count, dtype=jnp.int32)[:, None]
    key_pos = jnp.arange(2 * row_count, dtype=jnp.int32)[None, :]
    inside = (key_pos > query_pos) & (key_pos <= query_pos + row_count)
    block_ids = jnp.arange(block_count, dtype=jnp.int32)
    rim_open = (block_ids > 0) | (ctx_index != 0)
    allowed = inside[None, None] & (
        rim_open[:, None, None, None] | (key_pos >= row_count)[None, None]
    )
    scores = jnp.where(allowed, scores, -jnp.inf)
    largest = jnp.max(scores, axis=-1, keepdims=True)
    powers = jnp.exp(scores - largest)
    attn_weights = (powers / jnp.sum(powers, axis=-1, keepdims=True)).astype(jnp.bfloat16)
    attended = jnp.einsum(
        "chqk,ckhd->cqhd", attn_weights, window_values, preferred_element_type=jnp.float32
    )
    fast_stack = jnp.stack(fast_outputs)
    combined = (
        normalize_rms(fast_stack, 1e-05) * out_gain.reshape(local_heads, head_width) + attended
    ).astype(jnp.bfloat16)
    flat_rows = combined.reshape(block_count * row_count, local_heads * head_width)
    partial_out = jnp.dot(flat_rows, out_weight, preferred_element_type=jnp.float32)
    mixed_share = lax.psum_scatter(
        partial_out.astype(jnp.bfloat16), "head", scatter_dimension=1, tiled=True
    )
    layer_out = mixed_share.reshape(1, block_count, row_count, -1)
    piece = lax.all_gather(cotangent, "head", axis=3, tiled=True)
    grad_rows = jnp.einsum(
        "ti,tj->ij",
        flat_rows,
        piece.reshape(-1, piece.shape[3]),
        preferred_element_type=jnp.float32,
    )
    weight_grad = lax.psum_scatter(
        grad_rows.astype(jnp.bfloat16), ("seq", "ctx"), scatter_dimension=1, tiled=True
    ).astype(jnp.float32)
    return (layer_out, weight_grad, weight_in[None], weight_gate[None], weight_out[None])

BF = jnp.bfloat16
F32 = jnp.float32


def mm(left, right):
    return jnp.dot(left, right, preferred_element_type=F32)


def mm_tn(left, right):
    return lax.dot_general(left, right, (((0,), (0,)), ((), ())), preferred_element_type=F32)


def mm_nt(left, right):
    return lax.dot_general(left, right, (((1,), (1,)), ((), ())), preferred_element_type=F32)


def layer_kernel(
    seqs,
    heads,
    q_ref,
    k_ref,
    v_ref,
    rate_ref,
    win_ref,
    wgate_ref,
    wout_ref,
    gain_ref,
    ow_ref,
    cot_ref,
    out_ref,
    grad_ref,
    fin_ref,
    fgate_ref,
    fout_ref,
    qh,
    kh,
    vh,
    svh,
    sv_all,
    cot_all,
    rin,
    rgate,
    rout,
    acc_in,
    acc_gate,
    acc_out,
    fast,
    comb,
    comb_t,
    own,
    part,
    up_buf,
    down_buf,
    gsend,
    grecv,
    core_s,
    core_r,
    cot_core_s,
    cot_core_r,
    ag_up_s,
    ag_down_s,
    ag_r,
    comb_s,
    comb_r,
    fin_s,
    fin_r,
    up_s,
    up_r,
    down_s,
    down_r,
    g_s,
    g_r,
    local_s,
):
    s = lax.axis_index("seq")
    c = lax.axis_index("ctx")
    h = lax.axis_index("head")
    o = 1 - c
    blocks, rows = q_ref.shape[1], q_ref.shape[2]
    dh = win_ref.shape[1]
    mine = pl.ds(pl.multiple_of(c * dh, dh), dh)
    theirs = pl.ds(pl.multiple_of(o * dh, dh), dh)
    last = heads - 1

    def remote(src, dst, send, recv, where):
        return pltpu.make_async_remote_copy(
            src_ref=src,
            dst_ref=dst,
            send_sem=send,
            recv_sem=recv,
            device_id=where,
            device_id_type=pl.DeviceIdType.MESH,
        )

    barrier = pltpu.get_barrier_semaphore()
    for s2 in range(seqs):
        for c2 in range(2):

            @pl.when((s2 != s) | (c2 != c))
            def _():
                pl.semaphore_signal(
                    barrier,
                    inc=1,
                    device_id={"seq": s2, "ctx": c2},
                    device_id_type=pl.DeviceIdType.MESH,
                )

    @pl.when(h < last)
    def _():
        pl.semaphore_signal(
            barrier, inc=1, device_id={"head": h + 1}, device_id_type=pl.DeviceIdType.MESH
        )

    @pl.when(h > 0)
    def _():
        pl.semaphore_signal(
            barrier, inc=1, device_id={"head": h - 1}, device_id_type=pl.DeviceIdType.MESH
        )

    ends = (h == 0).astype(jnp.int32) + (h == last).astype(jnp.int32)
    pl.semaphore_wait(barrier, 2 * seqs - 1 + 2 - ends)

    def cot_up(owner, src):
        return remote(
            src, cot_all.at[owner, :, c], ag_up_s.at[owner], ag_r.at[owner], {"head": h + 1}
        )

    def cot_down(owner, src):
        return remote(
            src, cot_all.at[owner, :, c], ag_down_s.at[owner], ag_r.at[owner], {"head": h - 1}
        )

    def cot_core(owner, src):
        return remote(
            src, cot_all.at[owner, :, c], cot_core_s.at[owner], cot_core_r.at[owner], {"ctx": o}
        )

    def exchange(index, src, dst):
        return remote(src, dst, core_s.at[index], core_r.at[index], {"ctx": o})

    swaps = [
        exchange(0, k_ref.at[0, :, :, theirs], kh.at[:, c]),
        exchange(1, sv_all.at[:, :, theirs], svh.at[:, c]),
        exchange(2, q_ref.at[0, :, :, theirs], qh.at[:, c]),
        exchange(3, v_ref.at[0, :, :, theirs], vh.at[:, c]),
    ]
    swaps[0].start()
    swaps[2].start()
    swaps[3].start()

    @pl.when(h < last)
    def _():
        cot_up(h, cot_ref.at[0]).start()

    @pl.when(h > 0)
    def _():
        cot_down(h, cot_ref.at[0]).start()

    for b in range(blocks):
        for i in range(2):
            cols = slice(i * dh, (i + 1) * dh)
            rate = rate_ref[0, b, :, i : i + 1]
            sv_all[b, :, cols] = (rate * v_ref[0, b, :, cols].astype(F32)).astype(BF)
    swaps[1].start()
    cot_core(h, cot_ref.at[0]).start()
    locals_ = [
        pltpu.make_async_copy(k_ref.at[0, :, :, mine], kh.at[:, c], local_s.at[0]),
        pltpu.make_async_copy(sv_all.at[:, :, mine], svh.at[:, c], local_s.at[1]),
        pltpu.make_async_copy(q_ref.at[0, :, :, mine], qh.at[:, c], local_s.at[2]),
        pltpu.make_async_copy(v_ref.at[0, :, :, mine], vh.at[:, c], local_s.at[3]),
        pltpu.make_async_copy(cot_ref.at[0], cot_all.at[h, :, c], local_s.at[4]),
    ]
    for copy in locals_:
        copy.start()

    def squares(weight):
        return jnp.sum(weight * weight, axis=0, keepdims=True) + 1e-06

    targets = []
    for src, kept in ((win_ref, rin), (wgate_ref, rgate), (wout_ref, rout)):
        kept[...] = src[c]
        targets.append(jnp.sqrt(squares(src[c].astype(F32))))
    for copy in locals_:
        copy.wait()
    for copy in swaps:
        copy.wait()

    def fast_block(b):
        @pl.loop(0, 2)
        def _(i):
            key_norm = normalize_rms(kh[b, i].astype(F32), 1e-05).astype(BF)
            key_in = mm(key_norm, rin[...])
            key_gate = mm(key_norm, rgate[...])
            scaled = svh[b, i]
            d_feature = mm_nt(scaled, rout[...])
            sigma = jax.nn.sigmoid(key_in)
            active = key_in * sigma
            feature = (active * key_gate).astype(BF)
            d_in = (d_feature * key_gate * sigma * (1.0 + key_in * (1.0 - sigma))).astype(BF)
            d_gate = (d_feature * active).astype(BF)
            up_in = mm_tn(key_norm, d_in)
            up_gate = mm_tn(key_norm, d_gate)
            up_out = mm_tn(feature, scaled)

            @pl.when(i == 0)
            def _():
                acc_in[...] = up_in
                acc_gate[...] = up_gate
                acc_out[...] = up_out

            @pl.when(i == 1)
            def _():
                acc_in[...] += up_in
                acc_gate[...] += up_gate
                acc_out[...] += up_out

            query_norm = normalize_rms(qh[b, i].astype(F32), 1e-05).astype(BF)
            first = mm(query_norm, rin[...])
            hidden = (first * jax.nn.sigmoid(first) * mm(query_norm, rgate[...])).astype(BF)
            fast[i] = mm(hidden, rout[...])

        for kept, acc, final, target, start in (
            (rin, acc_in, fin_ref, targets[0], win_ref),
            (rgate, acc_gate, fgate_ref, targets[1], wgate_ref),
            (rout, acc_out, fout_ref, targets[2], wout_ref),
        ):
            weight = (start[c].astype(F32) if b == 0 else final[0, c]) + acc[...]
            weight = weight * (target / jnp.sqrt(squares(weight)))
            final[0, c] = weight
            kept[...] = weight.astype(BF)

    row = lax.broadcasted_iota(jnp.int32, (rows, rows), 0)
    col = lax.broadcasted_iota(jnp.int32, (rows, rows), 1)
    scale = 1.0 / math.sqrt(dh)

    def attend(b, i):
        query = qh[b, i]
        now = jnp.where(col <= row, mm_nt(query, kh[b, i]) * scale, -jnp.inf)
        largest = jnp.max(now, axis=-1, keepdims=True)
        if b == 0 and i == 0:
            powers = jnp.exp(now - largest)
            total = jnp.sum(powers, axis=-1, keepdims=True)
            return mm((powers / total).astype(BF), vh[b, i])
        before = (b, 0) if i == 1 else (b - 1, 1)
        old = jnp.where(col > row, mm_nt(query, kh[before]) * scale, -jnp.inf)
        largest = jnp.maximum(largest, jnp.max(old, axis=-1, keepdims=True))
        powers = jnp.exp(now - largest)
        old_powers = jnp.exp(old - largest)
        total = jnp.sum(powers, axis=-1, keepdims=True) + jnp.sum(
            old_powers, axis=-1, keepdims=True
        )
        return mm((powers / total).astype(BF), vh[b, i]) + mm(
            (old_powers / total).astype(BF), vh[before]
        )

    def comb_copy(b):
        return remote(
            comb.at[b, o], own.at[b, :, mine], comb_s.at[b], comb_r.at[b], {"ctx": o}
        )

    def combine(b):
        for i in range(2):
            value = (
                normalize_rms(fast[i], 1e-05) * gain_ref[pl.ds(c, 1), :] + attend(b, i)
            ).astype(BF)
            comb[b, i] = value
            at = (b * 2 + i) * rows
            comb_t[:, at : at + rows] = value.T
        comb_copy(b).start()
        own[b, :, mine] = comb[b, c]

    width = ow_ref.shape[1] // heads

    def up_copy(b, d):
        return remote(
            part.at[b, d], up_buf.at[b, d], up_s.at[b, d], up_r.at[b, d], {"head": h + 1}
        )

    def down_copy(b, d):
        return remote(
            part.at[b, d], down_buf.at[b, d], down_s.at[b, d], down_r.at[b, d], {"head": h - 1}
        )

    def project(b):
        comb_copy(b).wait()
        rows_in = own[b]
        for d in range(heads):
            part[b, d] = mm(rows_in, ow_ref[:, d * width : (d + 1) * width]).astype(BF)

        @pl.when(h == 0)
        def _():
            for d in range(last, 0, -1):
                up_copy(b, d).start()

        @pl.when(h == last)
        def _():
            for d in range(last):
                down_copy(b, d).start()

    def add(b, d, buf):
        part[b, d] = (part[b, d].astype(F32) + buf[b, d].astype(F32)).astype(BF)

    def forward(b):
        for step in range(heads - 2):
            d = last - step

            @pl.when((h > 0) & (h < d))
            def _(d=d):
                up_copy(b, d).wait_recv()
                add(b, d, up_buf)
                up_copy(b, d).start()

            e = step

            @pl.when((h < last) & (h > e))
            def _(e=e):
                down_copy(b, e).wait_recv()
                add(b, e, down_buf)
                down_copy(b, e).start()

    def finish(b):
        @pl.when(h > 0)
        def _():
            up_copy(b, h).wait_recv()
            add(b, h, up_buf)

        @pl.when(h < last)
        def _():
            down_copy(b, h).wait_recv()
            add(b, h, down_buf)

        out_ref[0, b] = part[b, h]
        for d in range(heads):

            @pl.when(d > h)
            def _(d=d):
                up_copy(b, d).wait_send()

            @pl.when(d < h)
            def _(d=d):
                down_copy(b, d).wait_send()

    def gather_step(t):
        @pl.when(h - t >= 0)
        def _():
            owner = h - t
            piece = cot_all.at[owner, :, c]
            cot_up(owner, piece).wait_recv()
            cot_core(owner, piece).start()

            @pl.when(h < last)
            def _():
                cot_up(owner, piece).start()

        @pl.when(h + t <= last)
        def _():
            owner = h + t
            piece = cot_all.at[owner, :, c]
            cot_down(owner, piece).wait_recv()
            cot_core(owner, piece).start()

            @pl.when(h > 0)
            def _():
                cot_down(owner, piece).start()

    def g_copy(j, c2):
        return remote(
            gsend.at[j, c2],
            grecv.at[s, c],
            g_s.at[j, c2],
            g_r.at[s, c],
            {"seq": j, "ctx": c2},
        )

    def grad_piece(j):
        cot_core(j, cot_all.at[j, :, c]).wait_recv()
        for c2 in range(2):
            block = cot_all[j, :, :, :, c2 * rows : (c2 + 1) * rows].reshape(-1, rows)
            gsend[j, c2] = mm(comb_t[...], block).astype(BF)

            @pl.when((j != s) | (c2 != c))
            def _(c2=c2):
                g_copy(j, c2).start()

            @pl.when((j == s) & (c2 == c))
            def _(c2=c2):
                grecv[s, c] = gsend[s, c2]

    def grad_step(t):
        @pl.when(h - t >= 0)
        def _():
            grad_piece(h - t)

        if t > 0:

            @pl.when(h + t <= last)
            def _():
                grad_piece(h + t)

    def fin_copy(index, ref):
        return remote(ref.at[0, c], ref.at[0, c], fin_s.at[index], fin_r.at[index], {"ctx": o})

    finals = [fin_copy(n, ref) for n, ref in enumerate((fin_ref, fgate_ref, fout_ref))]

    fast_block(0)
    combine(0)
    gather_step(1)
    project(0)
    fast_block(1)
    for copy in finals:
        copy.start()
    combine(1)
    forward(0)
    project(1)
    grad_step(0)
    for t in range(2, heads):
        gather_step(t)
        if t == 2:
            forward(1)
        grad_step(t - 1)
    grad_step(heads - 1)
    for b in range(blocks):
        finish(b)
    for copy in finals:
        copy.wait()
    for s2 in range(seqs):
        for c2 in range(2):

            @pl.when((s2 != s) | (c2 != c))
            def _(s2=s2, c2=c2):
                remote(
                    gsend.at[s2, c2],
                    grecv.at[s2, c2],
                    g_s.at[s2, c2],
                    g_r.at[s2, c2],
                    {"ctx": o},
                ).wait()

    for i in range(2):
        total = grecv[0, i].astype(F32)
        for s2 in range(1, seqs):
            total = total + grecv[s2, i].astype(F32)
        grad_ref[i * dh : (i + 1) * dh, :] = total
    for j in range(heads):
        piece = cot_all.at[j, :, c]
        cot_core(j, piece).wait_send()

        @pl.when((j <= h) & (h < last))
        def _(j=j, piece=piece):
            cot_up(j, piece).wait_send()

        @pl.when((j >= h) & (h > 0))
        def _(j=j, piece=piece):
            cot_down(j, piece).wait_send()


def fused_shards(
    queries,
    key_vectors,
    value_vectors,
    token_rates,
    fast_in,
    fast_gate,
    fast_out,
    out_gain,
    out_weight,
    cotangent,
):
    seqs, heads = lax.axis_size("seq"), lax.axis_size("head")
    local_heads, dh, fh = fast_in.shape
    _, blocks, rows, width = queries.shape
    depth = out_weight.shape[1]
    vmem, dma = pltpu.VMEM, pltpu.SemaphoreType.DMA
    whole = pl.BlockSpec(memory_space=pltpu.VMEM)
    return pl.pallas_call(
        functools.partial(layer_kernel, seqs, heads),
        out_shape=(
            jax.ShapeDtypeStruct((1, blocks, rows, width), BF),
            jax.ShapeDtypeStruct((width, rows), F32),
            jax.ShapeDtypeStruct((1, local_heads, dh, fh), F32),
            jax.ShapeDtypeStruct((1, local_heads, dh, fh), F32),
            jax.ShapeDtypeStruct((1, local_heads, fh, dh), F32),
        ),
        in_specs=[whole] * 10,
        out_specs=(whole,) * 5,
        scratch_shapes=[
            vmem((blocks, 2, rows, dh), BF),
            vmem((blocks, 2, rows, dh), BF),
            vmem((blocks, 2, rows, dh), BF),
            vmem((blocks, 2, rows, dh), BF),
            vmem((blocks, rows, width), BF),
            vmem((heads, blocks, 2, rows, width), BF),
            vmem((dh, fh), BF),
            vmem((dh, fh), BF),
            vmem((fh, dh), BF),
            vmem((dh, fh), F32),
            vmem((dh, fh), F32),
            vmem((fh, dh), F32),
            vmem((2, rows, dh), F32),
            vmem((blocks, 2, rows, dh), BF),
            vmem((dh, blocks * 2 * rows), BF),
            vmem((blocks, rows, width), BF),
            vmem((blocks, heads, rows, width), BF),
            vmem((blocks, heads, rows, width), BF),
            vmem((blocks, heads, rows, width), BF),
            vmem((heads, 2, dh, rows), BF),
            vmem((seqs, 2, dh, rows), BF),
            dma((4,)),
            dma((4,)),
            dma((heads,)),
            dma((heads,)),
            dma((heads,)),
            dma((heads,)),
            dma((heads,)),
            dma((blocks,)),
            dma((blocks,)),
            dma((3,)),
            dma((3,)),
            dma((blocks, heads)),
            dma((blocks, heads)),
            dma((blocks, heads)),
            dma((blocks, heads)),
            dma((seqs, 2)),
            dma((seqs, 2)),
            dma((5,)),
        ],
        compiler_params=pltpu.CompilerParams(
            collective_id=0, has_side_effects=True, vmem_limit_bytes=48 * 2**20
        ),
        cost_estimate=pl.CostEstimate(
            flops=5 * 10**9, bytes_accessed=10 * 2**20, transcendentals=2 * 10**6
        ),
        name="layer",
    )(
        queries,
        key_vectors,
        value_vectors,
        token_rates,
        fast_in,
        fast_gate,
        fast_out,
        out_gain.reshape(local_heads, dh),
        out_weight,
        cotangent,
    )


def pick(mesh):
    fits = mesh.shape["ctx"] == 2 and mesh.shape["seq"] == mesh.shape["head"]

    def body(*args):
        local_heads, dh, _ = args[4].shape
        _, _, rows, width = args[0].shape
        square = dh == rows and width == 2 * rows and local_heads == 2
        return (fused_shards if fits and square else shards)(*args)

    return body


def solution(mesh):
    return jax.shard_map(
        pick(mesh),
        mesh=mesh,
        in_specs=(
            P("seq", None, "ctx", "head"),
            P("seq", None, "ctx", "head"),
            P("seq", None, "ctx", "head"),
            P("seq", None, "ctx", "head"),
            P("head", None, None),
            P("head", None, None),
            P("head", None, None),
            P("head"),
            P("head", None),
            P("seq", None, "ctx", "head"),
        ),
        out_specs=(
            P("seq", None, "ctx", "head"),
            P("head", ("seq", "ctx")),
            P("seq", "head", None, None),
            P("seq", "head", None, None),
            P("seq", "head", None, None),
        ),
        check_vma=False,
    )
```

```python
import functools
import math

import jax
import jax.numpy as jnp
from jax import lax
from jax.experimental import pallas as pl
from jax.experimental.pallas import tpu as pltpu
from jax.sharding import PartitionSpec as P


def passed_along(value, axis, steps):
    count = lax.axis_size(axis)
    pairs = [(source, (source + steps) % count) for source in range(count)]
    return lax.ppermute(value, axis, pairs)


def normalize_rms(values_in, epsilon):
    return values_in * lax.rsqrt(jnp.mean(values_in * values_in, axis=-1, keepdims=True) + epsilon)


def column_norms(weight):
    return jnp.sqrt(jnp.sum(weight * weight, axis=-2, keepdims=True) + 1e-06)


def renorm(weight, target):
    return weight * (target / jnp.sqrt(jnp.sum(weight * weight, axis=-2, keepdims=True) + 1e-06))


def shards(
    queries,
    key_vectors,
    value_vectors,
    token_rates,
    fast_in,
    fast_gate,
    fast_out,
    out_gain,
    out_weight,
    cotangent,
):
    local_heads, head_width, hidden_width = fast_in.shape
    block_count = queries.shape[1]
    row_count = queries.shape[2]
    ctx_index = lax.axis_index("ctx")
    query_rows = queries[0].reshape(block_count, row_count, local_heads, head_width)
    key_rows = key_vectors[0].reshape(block_count, row_count, local_heads, head_width)
    value_rows = value_vectors[0].reshape(block_count, row_count, local_heads, head_width)
    weight_in = fast_in.astype(jnp.float32)
    weight_gate = fast_gate.astype(jnp.float32)
    weight_out = fast_out.astype(jnp.float32)
    target_in = column_norms(weight_in)
    target_gate = column_norms(weight_gate)
    target_out = column_norms(weight_out)
    fast_outputs = []
    for block_index in range(block_count):
        query_norm = normalize_rms(query_rows[block_index].astype(jnp.float32), 1e-05).astype(
            jnp.bfloat16
        )
        key_norm = normalize_rms(key_rows[block_index].astype(jnp.float32), 1e-05).astype(
            jnp.bfloat16
        )
        round_in = weight_in.astype(jnp.bfloat16)
        round_gate = weight_gate.astype(jnp.bfloat16)
        round_out = weight_out.astype(jnp.bfloat16)
        hidden = (
            jax.nn.silu(
                jnp.einsum("thd,hdf->thf", query_norm, round_in, preferred_element_type=jnp.float32)
            )
            * jnp.einsum("thd,hdf->thf", query_norm, round_gate, preferred_element_type=jnp.float32)
        ).astype(jnp.bfloat16)
        fast_outputs.append(
            jnp.einsum("thf,hfd->thd", hidden, round_out, preferred_element_type=jnp.float32)
        )
        key_in = jnp.einsum("thd,hdf->thf", key_norm, round_in, preferred_element_type=jnp.float32)
        key_gate = jnp.einsum(
            "thd,hdf->thf", key_norm, round_gate, preferred_element_type=jnp.float32
        )
        sigmoid_in = jax.nn.sigmoid(key_in)
        active = key_in * sigmoid_in
        feature = (active * key_gate).astype(jnp.bfloat16)
        scaled_values = (
            token_rates[0, block_index][:, :, None] * value_rows[block_index].astype(jnp.float32)
        ).astype(jnp.bfloat16)
        d_feature = jnp.einsum(
            "thd,hfd->thf", scaled_values, round_out, preferred_element_type=jnp.float32
        )
        d_in = (d_feature * key_gate * sigmoid_in * (1.0 + key_in * (1.0 - sigmoid_in))).astype(
            jnp.bfloat16
        )
        d_gate = (d_feature * active).astype(jnp.bfloat16)
        update_in = jnp.einsum("thd,thf->hdf", key_norm, d_in, preferred_element_type=jnp.float32)
        update_gate = jnp.einsum(
            "thd,thf->hdf", key_norm, d_gate, preferred_element_type=jnp.float32
        )
        update_out = jnp.einsum(
            "thf,thd->hfd", feature, scaled_values, preferred_element_type=jnp.float32
        )
        total_in, total_gate, total_out = lax.psum((update_in, update_gate, update_out), "ctx")
        weight_in = renorm(weight_in + total_in, target_in)
        weight_gate = renorm(weight_gate + total_gate, target_gate)
        weight_out = renorm(weight_out + total_out, target_out)
    rim_keys, rim_values = passed_along((key_vectors[0], value_vectors[0]), "ctx", 1)
    earlier_keys = jnp.concatenate([jnp.zeros_like(rim_keys[:1]), rim_keys[:-1]], axis=0)
    earlier_values = jnp.concatenate([jnp.zeros_like(rim_values[:1]), rim_values[:-1]], axis=0)
    is_first = ctx_index == 0
    rim_keys = jnp.where(is_first, earlier_keys, rim_keys)
    rim_values = jnp.where(is_first, earlier_values, rim_values)
    window_keys = jnp.concatenate([rim_keys, key_vectors[0]], axis=1).reshape(
        block_count, 2 * row_count, local_heads, head_width
    )
    window_values = jnp.concatenate([rim_values, value_vectors[0]], axis=1).reshape(
        block_count, 2 * row_count, local_heads, head_width
    )
    scores = jnp.einsum(
        "cqhd,ckhd->chqk", query_rows, window_keys, preferred_element_type=jnp.float32
    ) * (1.0 / math.sqrt(head_width))
    query_pos = jnp.arange(row_count, dtype=jnp.int32)[:, None]
    key_pos = jnp.arange(2 * row_count, dtype=jnp.int32)[None, :]
    inside = (key_pos > query_pos) & (key_pos <= query_pos + row_count)
    block_ids = jnp.arange(block_count, dtype=jnp.int32)
    rim_open = (block_ids > 0) | (ctx_index != 0)
    allowed = inside[None, None] & (
        rim_open[:, None, None, None] | (key_pos >= row_count)[None, None]
    )
    scores = jnp.where(allowed, scores, -jnp.inf)
    largest = jnp.max(scores, axis=-1, keepdims=True)
    powers = jnp.exp(scores - largest)
    attn_weights = (powers / jnp.sum(powers, axis=-1, keepdims=True)).astype(jnp.bfloat16)
    attended = jnp.einsum(
        "chqk,ckhd->cqhd", attn_weights, window_values, preferred_element_type=jnp.float32
    )
    fast_stack = jnp.stack(fast_outputs)
    combined = (
        normalize_rms(fast_stack, 1e-05) * out_gain.reshape(local_heads, head_width) + attended
    ).astype(jnp.bfloat16)
    flat_rows = combined.reshape(block_count * row_count, local_heads * head_width)
    partial_out = jnp.dot(flat_rows, out_weight, preferred_element_type=jnp.float32)
    mixed_share = lax.psum_scatter(
        partial_out.astype(jnp.bfloat16), "head", scatter_dimension=1, tiled=True
    )
    layer_out = mixed_share.reshape(1, block_count, row_count, -1)
    piece = lax.all_gather(cotangent, "head", axis=3, tiled=True)
    grad_rows = jnp.einsum(
        "ti,tj->ij",
        flat_rows,
        piece.reshape(-1, piece.shape[3]),
        preferred_element_type=jnp.float32,
    )
    weight_grad = lax.psum_scatter(
        grad_rows.astype(jnp.bfloat16), ("seq", "ctx"), scatter_dimension=1, tiled=True
    ).astype(jnp.float32)
    return (layer_out, weight_grad, weight_in[None], weight_gate[None], weight_out[None])

BF = jnp.bfloat16
F32 = jnp.float32


def mm(left, right):
    return jnp.dot(left, right, preferred_element_type=F32)


def mm_tn(left, right):
    return lax.dot_general(left, right, (((0,), (0,)), ((), ())), preferred_element_type=F32)


def mm_nt(left, right):
    return lax.dot_general(left, right, (((1,), (1,)), ((), ())), preferred_element_type=F32)


def layer_kernel(
    seqs,
    heads,
    q_ref,
    k_ref,
    v_ref,
    rate_ref,
    win_ref,
    wgate_ref,
    wout_ref,
    gain_ref,
    ow_ref,
    cot_ref,
    out_ref,
    grad_ref,
    fin_ref,
    fgate_ref,
    fout_ref,
    qh,
    kh,
    vh,
    svh,
    sv_all,
    cot_all,
    rin,
    rgate,
    rout,
    acc_in,
    acc_gate,
    acc_out,
    fast,
    comb,
    comb_t,
    own,
    part,
    up_buf,
    down_buf,
    gsend,
    grecv,
    last_in,
    last_gate,
    last_out,
    layer,
    grad,
    v_own,
    weights_in,
    weights_gate,
    weights_out,
    ow_own,
    core_s,
    core_r,
    cot_core_s,
    cot_core_r,
    ag_up_s,
    ag_down_s,
    ag_r,
    comb_s,
    comb_r,
    fin_s,
    fin_r,
    up_s,
    up_r,
    down_s,
    down_r,
    g_s,
    g_r,
    local_s,
):
    s = lax.axis_index("seq")
    c = lax.axis_index("ctx")
    h = lax.axis_index("head")
    o = 1 - c
    blocks, rows = q_ref.shape[1], q_ref.shape[2]
    dh = win_ref.shape[1]
    mine = pl.ds(pl.multiple_of(c * dh, dh), dh)
    theirs = pl.ds(pl.multiple_of(o * dh, dh), dh)
    last = heads - 1

    def remote(src, dst, send, recv, where):
        return pltpu.make_async_remote_copy(
            src_ref=src,
            dst_ref=dst,
            send_sem=send,
            recv_sem=recv,
            device_id=where,
            device_id_type=pl.DeviceIdType.MESH,
        )

    fetches = [
        pltpu.make_async_copy(src, dst, local_s.at[n])
        for n, (src, dst) in enumerate(
            (
                (v_ref.at[0], v_own),
                (win_ref.at[c], weights_in),
                (wgate_ref.at[c], weights_gate),
                (wout_ref.at[c], weights_out),
                (ow_ref, ow_own),
            ),
            5,
        )
    ]
    for copy in fetches:
        copy.start()
    fetch_v, *fetch_weights, fetch_ow = fetches

    barrier = pltpu.get_barrier_semaphore()
    for s2 in range(seqs):
        for c2 in range(2):

            @pl.when((s2 != s) | (c2 != c))
            def _():
                pl.semaphore_signal(
                    barrier,
                    inc=1,
                    device_id={"seq": s2, "ctx": c2},
                    device_id_type=pl.DeviceIdType.MESH,
                )

    @pl.when(h < last)
    def _():
        pl.semaphore_signal(
            barrier, inc=1, device_id={"head": h + 1}, device_id_type=pl.DeviceIdType.MESH
        )

    @pl.when(h > 0)
    def _():
        pl.semaphore_signal(
            barrier, inc=1, device_id={"head": h - 1}, device_id_type=pl.DeviceIdType.MESH
        )

    ends = (h == 0).astype(jnp.int32) + (h == last).astype(jnp.int32)
    pl.semaphore_wait(barrier, 2 * seqs - 1 + 2 - ends)

    writes = []

    def write(src, dst, index):
        writes.append(pltpu.make_async_copy(src, dst, local_s.at[index]))
        writes[-1].start()

    def cot_up(owner, src):
        return remote(
            src, cot_all.at[owner, :, c], ag_up_s.at[owner], ag_r.at[owner], {"head": h + 1}
        )

    def cot_down(owner, src):
        return remote(
            src, cot_all.at[owner, :, c], ag_down_s.at[owner], ag_r.at[owner], {"head": h - 1}
        )

    def cot_core(owner, src):
        return remote(
            src, cot_all.at[owner, :, c], cot_core_s.at[owner], cot_core_r.at[owner], {"ctx": o}
        )

    def exchange(index, src, dst):
        return remote(src, dst, core_s.at[index], core_r.at[index], {"ctx": o})

    swaps = [
        exchange(0, k_ref.at[0, :, :, theirs], kh.at[:, c]),
        exchange(1, sv_all.at[:, :, theirs], svh.at[:, c]),
        exchange(2, q_ref.at[0, :, :, theirs], qh.at[:, c]),
        exchange(3, v_ref.at[0, :, :, theirs], vh.at[:, c]),
    ]
    swaps[0].start()
    swaps[2].start()
    swaps[3].start()

    @pl.when(h < last)
    def _():
        cot_up(h, cot_ref.at[0]).start()

    @pl.when(h > 0)
    def _():
        cot_down(h, cot_ref.at[0]).start()

    fetch_v.wait()
    for b in range(blocks):
        for i in range(2):
            cols = slice(i * dh, (i + 1) * dh)
            rate = jnp.broadcast_to(rate_ref[0, b, i : i + 1, :], (128, rows)).T[:, :1]
            sv_all[b, :, cols] = (rate * v_own[b, :, cols].astype(F32)).astype(BF)
    swaps[1].start()
    cot_core(h, cot_ref.at[0]).start()
    locals_ = [
        pltpu.make_async_copy(k_ref.at[0, :, :, mine], kh.at[:, c], local_s.at[0]),
        pltpu.make_async_copy(sv_all.at[:, :, mine], svh.at[:, c], local_s.at[1]),
        pltpu.make_async_copy(q_ref.at[0, :, :, mine], qh.at[:, c], local_s.at[2]),
        pltpu.make_async_copy(v_ref.at[0, :, :, mine], vh.at[:, c], local_s.at[3]),
        pltpu.make_async_copy(cot_ref.at[0], cot_all.at[h, :, c], local_s.at[4]),
    ]
    for copy in locals_:
        copy.start()

    def squares(weight):
        return jnp.sum(weight * weight, axis=0, keepdims=True) + 1e-06

    targets = []
    for copy in fetch_weights:
        copy.wait()
    for src, kept in ((weights_in, rin), (weights_gate, rgate), (weights_out, rout)):
        kept[...] = src[...]
        targets.append(jnp.sqrt(squares(src[...].astype(F32))))
    for copy in locals_:
        copy.wait()
    for copy in swaps:
        copy.wait()

    def fast_block(b):
        @pl.loop(0, 2)
        def _(i):
            key_norm = normalize_rms(kh[b, i].astype(F32), 1e-05).astype(BF)
            key_in = mm(key_norm, rin[...])
            key_gate = mm(key_norm, rgate[...])
            scaled = svh[b, i]
            d_feature = mm_nt(scaled, rout[...])
            sigma = jax.nn.sigmoid(key_in)
            active = key_in * sigma
            feature = (active * key_gate).astype(BF)
            d_in = (d_feature * key_gate * sigma * (1.0 + key_in * (1.0 - sigma))).astype(BF)
            d_gate = (d_feature * active).astype(BF)
            up_in = mm_tn(key_norm, d_in)
            up_gate = mm_tn(key_norm, d_gate)
            up_out = mm_tn(feature, scaled)

            @pl.when(i == 0)
            def _():
                acc_in[...] = up_in
                acc_gate[...] = up_gate
                acc_out[...] = up_out

            @pl.when(i == 1)
            def _():
                acc_in[...] += up_in
                acc_gate[...] += up_gate
                acc_out[...] += up_out

            query_norm = normalize_rms(qh[b, i].astype(F32), 1e-05).astype(BF)
            first = mm(query_norm, rin[...])
            hidden = (first * jax.nn.sigmoid(first) * mm(query_norm, rgate[...])).astype(BF)
            fast[i] = mm(hidden, rout[...])

        for kept, acc, final, target, start in (
            (rin, acc_in, last_in, targets[0], weights_in),
            (rgate, acc_gate, last_gate, targets[1], weights_gate),
            (rout, acc_out, last_out, targets[2], weights_out),
        ):
            weight = (start[...].astype(F32) if b == 0 else final[...]) + acc[...]
            weight = weight * (target / jnp.sqrt(squares(weight)))
            final[...] = weight
            kept[...] = weight.astype(BF)

    row = lax.broadcasted_iota(jnp.int32, (rows, rows), 0)
    col = lax.broadcasted_iota(jnp.int32, (rows, rows), 1)
    scale = 1.0 / math.sqrt(dh)

    def attend(b, i):
        query = qh[b, i]
        now = jnp.where(col <= row, mm_nt(query, kh[b, i]) * scale, -jnp.inf)
        largest = jnp.max(now, axis=-1, keepdims=True)
        if b == 0 and i == 0:
            powers = jnp.exp(now - largest)
            total = jnp.sum(powers, axis=-1, keepdims=True)
            return mm((powers / total).astype(BF), vh[b, i])
        before = (b, 0) if i == 1 else (b - 1, 1)
        old = jnp.where(col > row, mm_nt(query, kh[before]) * scale, -jnp.inf)
        largest = jnp.maximum(largest, jnp.max(old, axis=-1, keepdims=True))
        powers = jnp.exp(now - largest)
        old_powers = jnp.exp(old - largest)
        total = jnp.sum(powers, axis=-1, keepdims=True) + jnp.sum(
            old_powers, axis=-1, keepdims=True
        )
        return mm((powers / total).astype(BF), vh[b, i]) + mm(
            (old_powers / total).astype(BF), vh[before]
        )

    def comb_copy(b):
        return remote(
            comb.at[b, o], own.at[b, :, mine], comb_s.at[b], comb_r.at[b], {"ctx": o}
        )

    def combine(b):
        for i in range(2):
            value = (
                normalize_rms(fast[i], 1e-05) * gain_ref[:, mine] + attend(b, i)
            ).astype(BF)
            comb[b, i] = value
            at = (b * 2 + i) * rows
            comb_t[:, at : at + rows] = value.T
        comb_copy(b).start()
        own[b, :, mine] = comb[b, c]

    width = ow_own.shape[1] // heads

    def up_copy(b, d):
        return remote(
            part.at[b, d], up_buf.at[b, d], up_s.at[b, d], up_r.at[b, d], {"head": h + 1}
        )

    def down_copy(b, d):
        return remote(
            part.at[b, d], down_buf.at[b, d], down_s.at[b, d], down_r.at[b, d], {"head": h - 1}
        )

    def project(b):
        comb_copy(b).wait()
        rows_in = own[b]
        for d in range(heads):
            part[b, d] = mm(rows_in, ow_own[:, d * width : (d + 1) * width]).astype(BF)

        @pl.when(h == 0)
        def _():
            for d in range(last, 0, -1):
                up_copy(b, d).start()

        @pl.when(h == last)
        def _():
            for d in range(last):
                down_copy(b, d).start()

    def add(b, d, buf):
        part[b, d] = (part[b, d].astype(F32) + buf[b, d].astype(F32)).astype(BF)

    def forward(b):
        for step in range(1, last):
            d = last + h - step

            @pl.when((h > 0) & (d <= last))
            def _(d=d):
                up_copy(b, d).wait_recv()
                add(b, d, up_buf)
                up_copy(b, d).start()

            e = step - (last - h)

            @pl.when((h < last) & (e >= 0))
            def _(e=e):
                down_copy(b, e).wait_recv()
                add(b, e, down_buf)
                down_copy(b, e).start()

    def finish(b):
        @pl.when(h > 0)
        def _():
            up_copy(b, h).wait_recv()
            add(b, h, up_buf)

        @pl.when(h < last)
        def _():
            down_copy(b, h).wait_recv()
            add(b, h, down_buf)

        layer[b] = part[b, h]
        write(layer.at[b], out_ref.at[0, b], 13 + b)
        for d in range(heads):

            @pl.when(d > h)
            def _(d=d):
                up_copy(b, d).wait_send()

            @pl.when(d < h)
            def _(d=d):
                down_copy(b, d).wait_send()

    def gather_step(t):
        @pl.when(h - t >= 0)
        def _():
            owner = h - t
            piece = cot_all.at[owner, :, c]
            cot_up(owner, piece).wait_recv()
            cot_core(owner, piece).start()

            @pl.when(h < last)
            def _():
                cot_up(owner, piece).start()

        @pl.when(h + t <= last)
        def _():
            owner = h + t
            piece = cot_all.at[owner, :, c]
            cot_down(owner, piece).wait_recv()
            cot_core(owner, piece).start()

            @pl.when(h > 0)
            def _():
                cot_down(owner, piece).start()

    def g_copy(j, c2):
        return remote(
            gsend.at[j, c2],
            grecv.at[s, c],
            g_s.at[j, c2],
            g_r.at[s, c],
            {"seq": j, "ctx": c2},
        )

    def grad_piece(j):
        cot_core(j, cot_all.at[j, :, c]).wait_recv()
        for c2 in range(2):
            block = cot_all[j, :, :, :, c2 * rows : (c2 + 1) * rows].reshape(-1, rows)
            gsend[j, c2] = mm(comb_t[...], block).astype(BF)

            @pl.when((j != s) | (c2 != c))
            def _(c2=c2):
                g_copy(j, c2).start()

            @pl.when((j == s) & (c2 == c))
            def _(c2=c2):
                grecv[s, c] = gsend[s, c2]

    def grad_step(t):
        @pl.when(h - t >= 0)
        def _():
            grad_piece(h - t)

        if t > 0:

            @pl.when(h + t <= last)
            def _():
                grad_piece(h + t)

    results = ((last_in, fin_ref), (last_gate, fgate_ref), (last_out, fout_ref))
    finals = [
        remote(src, dst.at[0, c], fin_s.at[n], fin_r.at[n], {"ctx": o})
        for n, (src, dst) in enumerate(results)
    ]

    fast_block(0)
    combine(0)
    gather_step(1)
    fetch_ow.wait()
    project(0)
    fast_block(1)
    for copy in finals:
        copy.start()
    for n, (src, dst) in enumerate(results):
        write(src, dst.at[0, c], 10 + n)
    combine(1)
    project(1)
    grad_step(0)
    for t in range(2, heads):
        grad_step(t - 1)
        gather_step(t)
        if t == 2:
            forward(0)
            forward(1)
    grad_step(heads - 1)
    for b in range(blocks):
        finish(b)
    for copy in finals:
        copy.wait()
    for s2 in range(seqs):
        for c2 in range(2):

            @pl.when((s2 != s) | (c2 != c))
            def _(s2=s2, c2=c2):
                remote(
                    gsend.at[s2, c2],
                    grecv.at[s2, c2],
                    g_s.at[s2, c2],
                    g_r.at[s2, c2],
                    {"ctx": o},
                ).wait()

    for i in range(2):
        span = pl.ds(i * dh, dh)
        total = grecv[0, i].astype(F32)
        for s2 in range(1, seqs):
            total = total + grecv[s2, i].astype(F32)
        grad[span, :] = total
        write(grad.at[span, :], grad_ref.at[span, :], 13 + blocks + i)
    for j in range(heads):
        piece = cot_all.at[j, :, c]
        cot_core(j, piece).wait_send()

        @pl.when((j <= h) & (h < last))
        def _(j=j, piece=piece):
            cot_up(j, piece).wait_send()

        @pl.when((j >= h) & (h > 0))
        def _(j=j, piece=piece):
            cot_down(j, piece).wait_send()

    for copy in writes:
        copy.wait()


def write_kernel(*refs):
    count = len(refs) // 2
    sources, targets, sems = refs[:count], refs[count:-1], refs[-1]
    copies = []
    for src, dst in zip(sources, targets):
        if len(src.shape) == 2:
            span = src.shape[0] // 2
            parts = [pl.ds(i * span, span) for i in range(2)]
        else:
            parts = [(0, i) for i in range(2)]
        for at in parts:
            one, other = src.at[at], dst.at[at]
            copies.append(pltpu.make_async_copy(one, other, sems.at[len(copies)]))
            copies[-1].start()
    for copy in copies:
        copy.wait()


def fused_shards(
    queries,
    key_vectors,
    value_vectors,
    token_rates,
    fast_in,
    fast_gate,
    fast_out,
    out_gain,
    out_weight,
    cotangent,
):
    seqs, heads = lax.axis_size("seq"), lax.axis_size("head")
    local_heads, dh, fh = fast_in.shape
    _, blocks, rows, width = queries.shape
    depth = out_weight.shape[1]
    vmem, dma = pltpu.VMEM, pltpu.SemaphoreType.DMA
    whole = pl.BlockSpec(memory_space=pltpu.VMEM)
    hbm = pl.BlockSpec(memory_space=pl.ANY)
    shapes = (
        jax.ShapeDtypeStruct((1, blocks, rows, width), BF),
        jax.ShapeDtypeStruct((width, rows), F32),
        jax.ShapeDtypeStruct((1, local_heads, dh, fh), F32),
        jax.ShapeDtypeStruct((1, local_heads, dh, fh), F32),
        jax.ShapeDtypeStruct((1, local_heads, fh, dh), F32),
    )
    results = pl.pallas_call(
        functools.partial(layer_kernel, seqs, heads),
        out_shape=shapes,
        in_specs=[hbm, hbm, hbm, whole, hbm, hbm, hbm, whole, hbm, hbm],
        out_specs=(hbm,) * 5,
        scratch_shapes=[
            vmem((blocks, 2, rows, dh), BF),
            vmem((blocks, 2, rows, dh), BF),
            vmem((blocks, 2, rows, dh), BF),
            vmem((blocks, 2, rows, dh), BF),
            vmem((blocks, rows, width), BF),
            vmem((heads, blocks, 2, rows, width), BF),
            vmem((dh, fh), BF),
            vmem((dh, fh), BF),
            vmem((fh, dh), BF),
            vmem((dh, fh), F32),
            vmem((dh, fh), F32),
            vmem((fh, dh), F32),
            vmem((2, rows, dh), F32),
            vmem((blocks, 2, rows, dh), BF),
            vmem((dh, blocks * 2 * rows), BF),
            vmem((blocks, rows, width), BF),
            vmem((blocks, heads, rows, width), BF),
            vmem((blocks, heads, rows, width), BF),
            vmem((blocks, heads, rows, width), BF),
            vmem((heads, 2, dh, rows), BF),
            vmem((seqs, 2, dh, rows), BF),
            vmem((dh, fh), F32),
            vmem((dh, fh), F32),
            vmem((fh, dh), F32),
            vmem((blocks, rows, width), BF),
            vmem((width, rows), F32),
            vmem((blocks, rows, width), BF),
            vmem((dh, fh), BF),
            vmem((dh, fh), BF),
            vmem((fh, dh), BF),
            vmem((width, depth), BF),
            dma((4,)),
            dma((4,)),
            dma((heads,)),
            dma((heads,)),
            dma((heads,)),
            dma((heads,)),
            dma((heads,)),
            dma((blocks,)),
            dma((blocks,)),
            dma((3,)),
            dma((3,)),
            dma((blocks, heads)),
            dma((blocks, heads)),
            dma((blocks, heads)),
            dma((blocks, heads)),
            dma((seqs, 2)),
            dma((seqs, 2)),
            dma((15 + blocks,)),
        ],
        compiler_params=pltpu.CompilerParams(
            collective_id=0, has_side_effects=True, vmem_limit_bytes=60 * 2**20
        ),
        cost_estimate=pl.CostEstimate(
            flops=5 * 10**9, bytes_accessed=10 * 2**20, transcendentals=2 * 10**6
        ),
        name="layer",
    )(
        queries,
        key_vectors,
        value_vectors,
        jnp.swapaxes(token_rates, 2, 3),
        fast_in,
        fast_gate,
        fast_out,
        out_gain.reshape(1, width),
        out_weight,
        cotangent,
    )
    return pl.pallas_call(
        write_kernel,
        out_shape=shapes,
        in_specs=[hbm] * 5,
        out_specs=(hbm,) * 5,
        scratch_shapes=[dma((10,))],
        compiler_params=pltpu.CompilerParams(vmem_limit_bytes=60 * 2**20),
        name="write",
    )(*results)


def pick(mesh):
    fits = mesh.shape["ctx"] == 2 and mesh.shape["seq"] == mesh.shape["head"]

    def body(*args):
        local_heads, dh, _ = args[4].shape
        _, _, rows, width = args[0].shape
        square = dh == rows and width == 2 * rows and local_heads == 2 and args[0].shape[1] == 2
        return (fused_shards if fits and square else shards)(*args)

    return body


def solution(mesh):
    return jax.shard_map(
        pick(mesh),
        mesh=mesh,
        in_specs=(
            P("seq", None, "ctx", "head"),
            P("seq", None, "ctx", "head"),
            P("seq", None, "ctx", "head"),
            P("seq", None, "ctx", "head"),
            P("head", None, None),
            P("head", None, None),
            P("head", None, None),
            P("head"),
            P("head", None),
            P("seq", None, "ctx", "head"),
        ),
        out_specs=(
            P("seq", None, "ctx", "head"),
            P("head", ("seq", "ctx")),
            P("seq", "head", None, None),
            P("seq", "head", None, None),
            P("seq", "head", None, None),
        ),
        check_vma=False,
    )
```

```python
import functools
import math

import jax
import jax.numpy as jnp
from jax import lax
from jax.experimental import pallas as pl
from jax.experimental.pallas import tpu as pltpu
from jax.sharding import PartitionSpec as P


def passed_along(value, axis, steps):
    count = lax.axis_size(axis)
    pairs = [(source, (source + steps) % count) for source in range(count)]
    return lax.ppermute(value, axis, pairs)


def normalize_rms(values_in, epsilon):
    return values_in * lax.rsqrt(jnp.mean(values_in * values_in, axis=-1, keepdims=True) + epsilon)


def column_norms(weight):
    return jnp.sqrt(jnp.sum(weight * weight, axis=-2, keepdims=True) + 1e-06)


def renorm(weight, target):
    return weight * (target / jnp.sqrt(jnp.sum(weight * weight, axis=-2, keepdims=True) + 1e-06))


def shards(
    queries,
    key_vectors,
    value_vectors,
    token_rates,
    fast_in,
    fast_gate,
    fast_out,
    out_gain,
    out_weight,
    cotangent,
):
    local_heads, head_width, hidden_width = fast_in.shape
    block_count = queries.shape[1]
    row_count = queries.shape[2]
    ctx_index = lax.axis_index("ctx")
    query_rows = queries[0].reshape(block_count, row_count, local_heads, head_width)
    key_rows = key_vectors[0].reshape(block_count, row_count, local_heads, head_width)
    value_rows = value_vectors[0].reshape(block_count, row_count, local_heads, head_width)
    weight_in = fast_in.astype(jnp.float32)
    weight_gate = fast_gate.astype(jnp.float32)
    weight_out = fast_out.astype(jnp.float32)
    target_in = column_norms(weight_in)
    target_gate = column_norms(weight_gate)
    target_out = column_norms(weight_out)
    fast_outputs = []
    for block_index in range(block_count):
        query_norm = normalize_rms(query_rows[block_index].astype(jnp.float32), 1e-05).astype(
            jnp.bfloat16
        )
        key_norm = normalize_rms(key_rows[block_index].astype(jnp.float32), 1e-05).astype(
            jnp.bfloat16
        )
        round_in = weight_in.astype(jnp.bfloat16)
        round_gate = weight_gate.astype(jnp.bfloat16)
        round_out = weight_out.astype(jnp.bfloat16)
        hidden = (
            jax.nn.silu(
                jnp.einsum("thd,hdf->thf", query_norm, round_in, preferred_element_type=jnp.float32)
            )
            * jnp.einsum("thd,hdf->thf", query_norm, round_gate, preferred_element_type=jnp.float32)
        ).astype(jnp.bfloat16)
        fast_outputs.append(
            jnp.einsum("thf,hfd->thd", hidden, round_out, preferred_element_type=jnp.float32)
        )
        key_in = jnp.einsum("thd,hdf->thf", key_norm, round_in, preferred_element_type=jnp.float32)
        key_gate = jnp.einsum(
            "thd,hdf->thf", key_norm, round_gate, preferred_element_type=jnp.float32
        )
        sigmoid_in = jax.nn.sigmoid(key_in)
        active = key_in * sigmoid_in
        feature = (active * key_gate).astype(jnp.bfloat16)
        scaled_values = (
            token_rates[0, block_index][:, :, None] * value_rows[block_index].astype(jnp.float32)
        ).astype(jnp.bfloat16)
        d_feature = jnp.einsum(
            "thd,hfd->thf", scaled_values, round_out, preferred_element_type=jnp.float32
        )
        d_in = (d_feature * key_gate * sigmoid_in * (1.0 + key_in * (1.0 - sigmoid_in))).astype(
            jnp.bfloat16
        )
        d_gate = (d_feature * active).astype(jnp.bfloat16)
        update_in = jnp.einsum("thd,thf->hdf", key_norm, d_in, preferred_element_type=jnp.float32)
        update_gate = jnp.einsum(
            "thd,thf->hdf", key_norm, d_gate, preferred_element_type=jnp.float32
        )
        update_out = jnp.einsum(
            "thf,thd->hfd", feature, scaled_values, preferred_element_type=jnp.float32
        )
        total_in, total_gate, total_out = lax.psum((update_in, update_gate, update_out), "ctx")
        weight_in = renorm(weight_in + total_in, target_in)
        weight_gate = renorm(weight_gate + total_gate, target_gate)
        weight_out = renorm(weight_out + total_out, target_out)
    rim_keys, rim_values = passed_along((key_vectors[0], value_vectors[0]), "ctx", 1)
    earlier_keys = jnp.concatenate([jnp.zeros_like(rim_keys[:1]), rim_keys[:-1]], axis=0)
    earlier_values = jnp.concatenate([jnp.zeros_like(rim_values[:1]), rim_values[:-1]], axis=0)
    is_first = ctx_index == 0
    rim_keys = jnp.where(is_first, earlier_keys, rim_keys)
    rim_values = jnp.where(is_first, earlier_values, rim_values)
    window_keys = jnp.concatenate([rim_keys, key_vectors[0]], axis=1).reshape(
        block_count, 2 * row_count, local_heads, head_width
    )
    window_values = jnp.concatenate([rim_values, value_vectors[0]], axis=1).reshape(
        block_count, 2 * row_count, local_heads, head_width
    )
    scores = jnp.einsum(
        "cqhd,ckhd->chqk", query_rows, window_keys, preferred_element_type=jnp.float32
    ) * (1.0 / math.sqrt(head_width))
    query_pos = jnp.arange(row_count, dtype=jnp.int32)[:, None]
    key_pos = jnp.arange(2 * row_count, dtype=jnp.int32)[None, :]
    inside = (key_pos > query_pos) & (key_pos <= query_pos + row_count)
    block_ids = jnp.arange(block_count, dtype=jnp.int32)
    rim_open = (block_ids > 0) | (ctx_index != 0)
    allowed = inside[None, None] & (
        rim_open[:, None, None, None] | (key_pos >= row_count)[None, None]
    )
    scores = jnp.where(allowed, scores, -jnp.inf)
    largest = jnp.max(scores, axis=-1, keepdims=True)
    powers = jnp.exp(scores - largest)
    attn_weights = (powers / jnp.sum(powers, axis=-1, keepdims=True)).astype(jnp.bfloat16)
    attended = jnp.einsum(
        "chqk,ckhd->cqhd", attn_weights, window_values, preferred_element_type=jnp.float32
    )
    fast_stack = jnp.stack(fast_outputs)
    combined = (
        normalize_rms(fast_stack, 1e-05) * out_gain.reshape(local_heads, head_width) + attended
    ).astype(jnp.bfloat16)
    flat_rows = combined.reshape(block_count * row_count, local_heads * head_width)
    partial_out = jnp.dot(flat_rows, out_weight, preferred_element_type=jnp.float32)
    mixed_share = lax.psum_scatter(
        partial_out.astype(jnp.bfloat16), "head", scatter_dimension=1, tiled=True
    )
    layer_out = mixed_share.reshape(1, block_count, row_count, -1)
    piece = lax.all_gather(cotangent, "head", axis=3, tiled=True)
    grad_rows = jnp.einsum(
        "ti,tj->ij",
        flat_rows,
        piece.reshape(-1, piece.shape[3]),
        preferred_element_type=jnp.float32,
    )
    weight_grad = lax.psum_scatter(
        grad_rows.astype(jnp.bfloat16), ("seq", "ctx"), scatter_dimension=1, tiled=True
    ).astype(jnp.float32)
    return (layer_out, weight_grad, weight_in[None], weight_gate[None], weight_out[None])

BF = jnp.bfloat16
F32 = jnp.float32


def mm(left, right):
    return jnp.dot(left, right, preferred_element_type=F32)


def mm_tn(left, right):
    return lax.dot_general(left, right, (((0,), (0,)), ((), ())), preferred_element_type=F32)


def mm_nt(left, right):
    return lax.dot_general(left, right, (((1,), (1,)), ((), ())), preferred_element_type=F32)


def layer_kernel(
    seqs,
    heads,
    q_ref,
    k_ref,
    v_ref,
    rate_ref,
    win_ref,
    wgate_ref,
    wout_ref,
    gain_ref,
    ow_ref,
    cot_ref,
    out_ref,
    grad_ref,
    fin_ref,
    fgate_ref,
    fout_ref,
    qh,
    kh,
    vh,
    svh,
    sv_all,
    cot_all,
    rin,
    rgate,
    rout,
    acc_in,
    acc_gate,
    acc_out,
    fast,
    comb,
    comb_t,
    own,
    part,
    up_buf,
    down_buf,
    gsend,
    grecv,
    last_in,
    last_gate,
    last_out,
    layer,
    grad,
    v_own,
    weights_in,
    weights_gate,
    weights_out,
    ow_own,
    core_s,
    core_r,
    cot_core_s,
    cot_core_r,
    ag_up_s,
    ag_down_s,
    ag_r,
    comb_s,
    comb_r,
    fin_s,
    fin_r,
    up_s,
    up_r,
    down_s,
    down_r,
    g_s,
    g_r,
    local_s,
):
    s = lax.axis_index("seq")
    c = lax.axis_index("ctx")
    h = lax.axis_index("head")
    o = 1 - c
    blocks, rows = q_ref.shape[1], q_ref.shape[2]
    dh = win_ref.shape[1]
    mine = pl.ds(pl.multiple_of(c * dh, dh), dh)
    theirs = pl.ds(pl.multiple_of(o * dh, dh), dh)
    last = heads - 1

    def remote(src, dst, send, recv, where):
        return pltpu.make_async_remote_copy(
            src_ref=src,
            dst_ref=dst,
            send_sem=send,
            recv_sem=recv,
            device_id=where,
            device_id_type=pl.DeviceIdType.MESH,
        )

    fetches = [
        pltpu.make_async_copy(src, dst, local_s.at[n])
        for n, (src, dst) in enumerate(
            (
                (v_ref.at[0], v_own),
                (win_ref.at[c], weights_in),
                (wgate_ref.at[c], weights_gate),
                (wout_ref.at[c], weights_out),
                (ow_ref, ow_own),
            ),
            5,
        )
    ]
    for copy in fetches:
        copy.start()
    fetch_v, *fetch_weights, fetch_ow = fetches

    barrier = pltpu.get_barrier_semaphore()
    for s2 in range(seqs):
        for c2 in range(2):

            @pl.when((s2 != s) | (c2 != c))
            def _():
                pl.semaphore_signal(
                    barrier,
                    inc=1,
                    device_id={"seq": s2, "ctx": c2},
                    device_id_type=pl.DeviceIdType.MESH,
                )

    @pl.when(h < last)
    def _():
        pl.semaphore_signal(
            barrier, inc=1, device_id={"head": h + 1}, device_id_type=pl.DeviceIdType.MESH
        )

    @pl.when(h > 0)
    def _():
        pl.semaphore_signal(
            barrier, inc=1, device_id={"head": h - 1}, device_id_type=pl.DeviceIdType.MESH
        )

    ends = (h == 0).astype(jnp.int32) + (h == last).astype(jnp.int32)
    pl.semaphore_wait(barrier, 2 * seqs - 1 + 2 - ends)

    writes = []

    def write(src, dst, index):
        writes.append(pltpu.make_async_copy(src, dst, local_s.at[index]))
        writes[-1].start()

    def cot_up(owner, src):
        return remote(
            src, cot_all.at[owner, :, c], ag_up_s.at[owner], ag_r.at[owner], {"head": h + 1}
        )

    def cot_down(owner, src):
        return remote(
            src, cot_all.at[owner, :, c], ag_down_s.at[owner], ag_r.at[owner], {"head": h - 1}
        )

    def cot_core(owner, src):
        return remote(
            src, cot_all.at[owner, :, c], cot_core_s.at[owner], cot_core_r.at[owner], {"ctx": o}
        )

    def exchange(index, src, dst):
        return remote(src, dst, core_s.at[index], core_r.at[index], {"ctx": o})

    swaps = [
        exchange(0, k_ref.at[0, :, :, theirs], kh.at[:, c]),
        exchange(1, sv_all.at[:, :, theirs], svh.at[:, c]),
        exchange(2, q_ref.at[0, :, :, theirs], qh.at[:, c]),
        exchange(3, v_ref.at[0, :, :, theirs], vh.at[:, c]),
    ]
    swaps[0].start()
    swaps[2].start()
    swaps[3].start()

    @pl.when(h < last)
    def _():
        cot_up(h, cot_ref.at[0]).start()

    @pl.when(h > 0)
    def _():
        cot_down(h, cot_ref.at[0]).start()

    fetch_v.wait()
    for b in range(blocks):
        for i in range(2):
            cols = slice(i * dh, (i + 1) * dh)
            rate = jnp.broadcast_to(rate_ref[0, b, i : i + 1, :], (128, rows)).T[:, :1]
            sv_all[b, :, cols] = (rate * v_own[b, :, cols].astype(F32)).astype(BF)
    swaps[1].start()
    cot_core(h, cot_ref.at[0]).start()
    locals_ = [
        pltpu.make_async_copy(k_ref.at[0, :, :, mine], kh.at[:, c], local_s.at[0]),
        pltpu.make_async_copy(sv_all.at[:, :, mine], svh.at[:, c], local_s.at[1]),
        pltpu.make_async_copy(q_ref.at[0, :, :, mine], qh.at[:, c], local_s.at[2]),
        pltpu.make_async_copy(v_ref.at[0, :, :, mine], vh.at[:, c], local_s.at[3]),
        pltpu.make_async_copy(cot_ref.at[0], cot_all.at[h, :, c], local_s.at[4]),
    ]
    for copy in locals_:
        copy.start()

    def squares(weight):
        return jnp.sum(weight * weight, axis=0, keepdims=True) + 1e-06

    targets = []
    for copy in fetch_weights:
        copy.wait()
    for src, kept in ((weights_in, rin), (weights_gate, rgate), (weights_out, rout)):
        kept[...] = src[...]
        targets.append(jnp.sqrt(squares(src[...].astype(F32))))
    for copy in locals_:
        copy.wait()
    for copy in swaps:
        copy.wait()

    def query_block(b):
        @pl.loop(0, 2)
        def _(i):
            query_norm = normalize_rms(qh[b, i].astype(F32), 1e-05).astype(BF)
            first = mm(query_norm, rin[...])
            hidden = (first * jax.nn.sigmoid(first) * mm(query_norm, rgate[...])).astype(BF)
            fast[i] = mm(hidden, rout[...])

    def key_block(b):
        @pl.loop(0, 2)
        def _(i):
            key_norm = normalize_rms(kh[b, i].astype(F32), 1e-05).astype(BF)
            key_in = mm(key_norm, rin[...])
            key_gate = mm(key_norm, rgate[...])
            scaled = svh[b, i]
            d_feature = mm_nt(scaled, rout[...])
            sigma = jax.nn.sigmoid(key_in)
            active = key_in * sigma
            feature = (active * key_gate).astype(BF)
            d_in = (d_feature * key_gate * sigma * (1.0 + key_in * (1.0 - sigma))).astype(BF)
            d_gate = (d_feature * active).astype(BF)
            up_in = mm_tn(key_norm, d_in)
            up_gate = mm_tn(key_norm, d_gate)
            up_out = mm_tn(feature, scaled)

            @pl.when(i == 0)
            def _():
                acc_in[...] = up_in
                acc_gate[...] = up_gate
                acc_out[...] = up_out

            @pl.when(i == 1)
            def _():
                acc_in[...] += up_in
                acc_gate[...] += up_gate
                acc_out[...] += up_out

        for kept, acc, final, target, start in (
            (rin, acc_in, last_in, targets[0], weights_in),
            (rgate, acc_gate, last_gate, targets[1], weights_gate),
            (rout, acc_out, last_out, targets[2], weights_out),
        ):
            weight = (start[...].astype(F32) if b == 0 else final[...]) + acc[...]
            weight = weight * (target / jnp.sqrt(squares(weight)))
            final[...] = weight
            kept[...] = weight.astype(BF)

    row = lax.broadcasted_iota(jnp.int32, (rows, rows), 0)
    col = lax.broadcasted_iota(jnp.int32, (rows, rows), 1)
    scale = 1.0 / math.sqrt(dh)

    def attend(b, i):
        query = qh[b, i]
        now = jnp.where(col <= row, mm_nt(query, kh[b, i]) * scale, -jnp.inf)
        largest = jnp.max(now, axis=-1, keepdims=True)
        if b == 0 and i == 0:
            powers = jnp.exp(now - largest)
            total = jnp.sum(powers, axis=-1, keepdims=True)
            return mm((powers / total).astype(BF), vh[b, i])
        before = (b, 0) if i == 1 else (b - 1, 1)
        old = jnp.where(col > row, mm_nt(query, kh[before]) * scale, -jnp.inf)
        largest = jnp.maximum(largest, jnp.max(old, axis=-1, keepdims=True))
        powers = jnp.exp(now - largest)
        old_powers = jnp.exp(old - largest)
        total = jnp.sum(powers, axis=-1, keepdims=True) + jnp.sum(
            old_powers, axis=-1, keepdims=True
        )
        return mm((powers / total).astype(BF), vh[b, i]) + mm(
            (old_powers / total).astype(BF), vh[before]
        )

    def comb_copy(b):
        return remote(
            comb.at[b, o], own.at[b, :, mine], comb_s.at[b], comb_r.at[b], {"ctx": o}
        )

    def combine(b):
        for i in range(2):
            value = (
                normalize_rms(fast[i], 1e-05) * gain_ref[:, mine] + attend(b, i)
            ).astype(BF)
            comb[b, i] = value
            at = (b * 2 + i) * rows
            comb_t[:, at : at + rows] = value.T
        comb_copy(b).start()
        own[b, :, mine] = comb[b, c]

    width = ow_own.shape[1] // heads

    def up_copy(b, d):
        return remote(
            part.at[b, d], up_buf.at[b, d], up_s.at[b, d], up_r.at[b, d], {"head": h + 1}
        )

    def down_copy(b, d):
        return remote(
            part.at[b, d], down_buf.at[b, d], down_s.at[b, d], down_r.at[b, d], {"head": h - 1}
        )

    def project(b):
        comb_copy(b).wait()
        rows_in = own[b]
        for d in range(heads):
            part[b, d] = mm(rows_in, ow_own[:, d * width : (d + 1) * width]).astype(BF)

        @pl.when(h == 0)
        def _():
            for d in range(last, 0, -1):
                up_copy(b, d).start()

        @pl.when(h == last)
        def _():
            for d in range(last):
                down_copy(b, d).start()

    def add(b, d, buf):
        part[b, d] = (part[b, d].astype(F32) + buf[b, d].astype(F32)).astype(BF)

    def forward(b):
        for step in range(1, last):
            d = last + h - step

            @pl.when((h > 0) & (d <= last))
            def _(d=d):
                up_copy(b, d).wait_recv()
                add(b, d, up_buf)
                up_copy(b, d).start()

            e = step - (last - h)

            @pl.when((h < last) & (e >= 0))
            def _(e=e):
                down_copy(b, e).wait_recv()
                add(b, e, down_buf)
                down_copy(b, e).start()

    def finish(b):
        @pl.when(h > 0)
        def _():
            up_copy(b, h).wait_recv()
            add(b, h, up_buf)

        @pl.when(h < last)
        def _():
            down_copy(b, h).wait_recv()
            add(b, h, down_buf)

        layer[b] = part[b, h]
        write(layer.at[b], out_ref.at[0, b], 13 + b)
        for d in range(heads):

            @pl.when(d > h)
            def _(d=d):
                up_copy(b, d).wait_send()

            @pl.when(d < h)
            def _(d=d):
                down_copy(b, d).wait_send()

    def gather_step(t):
        @pl.when(h - t >= 0)
        def _():
            owner = h - t
            piece = cot_all.at[owner, :, c]
            cot_up(owner, piece).wait_recv()
            cot_core(owner, piece).start()

            @pl.when(h < last)
            def _():
                cot_up(owner, piece).start()

        @pl.when(h + t <= last)
        def _():
            owner = h + t
            piece = cot_all.at[owner, :, c]
            cot_down(owner, piece).wait_recv()
            cot_core(owner, piece).start()

            @pl.when(h > 0)
            def _():
                cot_down(owner, piece).start()

    def g_copy(j, c2):
        return remote(
            gsend.at[j, c2],
            grecv.at[s, c],
            g_s.at[j, c2],
            g_r.at[s, c],
            {"seq": j, "ctx": c2},
        )

    def grad_piece(j):
        cot_core(j, cot_all.at[j, :, c]).wait_recv()
        for c2 in range(2):
            block = cot_all[j, :, :, :, c2 * rows : (c2 + 1) * rows].reshape(-1, rows)
            gsend[j, c2] = mm(comb_t[...], block).astype(BF)

            @pl.when((j != s) | (c2 != c))
            def _(c2=c2):
                g_copy(j, c2).start()

            @pl.when((j == s) & (c2 == c))
            def _(c2=c2):
                grecv[s, c] = gsend[s, c2]

    def grad_step(t):
        @pl.when(h - t >= 0)
        def _():
            grad_piece(h - t)

        if t > 0:

            @pl.when(h + t <= last)
            def _():
                grad_piece(h + t)

    results = ((last_in, fin_ref), (last_gate, fgate_ref), (last_out, fout_ref))
    finals = [
        remote(src, dst.at[0, c], fin_s.at[n], fin_r.at[n], {"ctx": o})
        for n, (src, dst) in enumerate(results)
    ]

    query_block(0)
    combine(0)
    fetch_ow.wait()
    project(0)
    key_block(0)
    gather_step(1)
    query_block(1)
    combine(1)
    project(1)
    grad_step(0)
    grad_step(1)
    key_block(1)
    for copy in finals:
        copy.start()
    for n, (src, dst) in enumerate(results):
        write(src, dst.at[0, c], 10 + n)
    for t in range(2, heads):
        gather_step(t)
        if t == 2:
            forward(0)
        grad_step(t)
        if t == 2:
            forward(1)
    for b in range(blocks):
        finish(b)
    for copy in finals:
        copy.wait()
    for s2 in range(seqs):
        for c2 in range(2):

            @pl.when((s2 != s) | (c2 != c))
            def _(s2=s2, c2=c2):
                remote(
                    gsend.at[s2, c2],
                    grecv.at[s2, c2],
                    g_s.at[s2, c2],
                    g_r.at[s2, c2],
                    {"ctx": o},
                ).wait()

    for i in range(2):
        span = pl.ds(i * dh, dh)
        total = grecv[0, i].astype(F32)
        for s2 in range(1, seqs):
            total = total + grecv[s2, i].astype(F32)
        grad[span, :] = total
        write(grad.at[span, :], grad_ref.at[span, :], 13 + blocks + i)
    for j in range(heads):
        piece = cot_all.at[j, :, c]
        cot_core(j, piece).wait_send()

        @pl.when((j <= h) & (h < last))
        def _(j=j, piece=piece):
            cot_up(j, piece).wait_send()

        @pl.when((j >= h) & (h > 0))
        def _(j=j, piece=piece):
            cot_down(j, piece).wait_send()

    for copy in writes:
        copy.wait()


def write_kernel(*refs):
    count = len(refs) // 3
    sems = refs[-1]
    reads, writes = [], []
    for src, dst, held in zip(refs[:count], refs[count : 2 * count], refs[2 * count : -1]):
        if len(src.shape) == 2:
            span = src.shape[0] // 2
            parts = [pl.ds(i * span, span) for i in range(2)]
        else:
            parts = [(0, i) for i in range(2)]
        for at in parts:
            n = len(reads)
            reads.append(pltpu.make_async_copy(src.at[at], held.at[at], sems.at[0, n]))
            writes.append(pltpu.make_async_copy(held.at[at], dst.at[at], sems.at[1, n]))
            reads[-1].start()
    for read, write in zip(reads, writes):
        read.wait()
        write.start()
    for write in writes:
        write.wait()


def fused_shards(
    queries,
    key_vectors,
    value_vectors,
    token_rates,
    fast_in,
    fast_gate,
    fast_out,
    out_gain,
    out_weight,
    cotangent,
):
    seqs, heads = lax.axis_size("seq"), lax.axis_size("head")
    local_heads, dh, fh = fast_in.shape
    _, blocks, rows, width = queries.shape
    depth = out_weight.shape[1]
    vmem, dma = pltpu.VMEM, pltpu.SemaphoreType.DMA
    whole = pl.BlockSpec(memory_space=pltpu.VMEM)
    hbm = pl.BlockSpec(memory_space=pl.ANY)
    shapes = (
        jax.ShapeDtypeStruct((1, blocks, rows, width), BF),
        jax.ShapeDtypeStruct((width, rows), F32),
        jax.ShapeDtypeStruct((1, local_heads, dh, fh), F32),
        jax.ShapeDtypeStruct((1, local_heads, dh, fh), F32),
        jax.ShapeDtypeStruct((1, local_heads, fh, dh), F32),
    )
    results = pl.pallas_call(
        functools.partial(layer_kernel, seqs, heads),
        out_shape=shapes,
        in_specs=[hbm, hbm, hbm, whole, hbm, hbm, hbm, whole, hbm, hbm],
        out_specs=(hbm,) * 5,
        scratch_shapes=[
            vmem((blocks, 2, rows, dh), BF),
            vmem((blocks, 2, rows, dh), BF),
            vmem((blocks, 2, rows, dh), BF),
            vmem((blocks, 2, rows, dh), BF),
            vmem((blocks, rows, width), BF),
            vmem((heads, blocks, 2, rows, width), BF),
            vmem((dh, fh), BF),
            vmem((dh, fh), BF),
            vmem((fh, dh), BF),
            vmem((dh, fh), F32),
            vmem((dh, fh), F32),
            vmem((fh, dh), F32),
            vmem((2, rows, dh), F32),
            vmem((blocks, 2, rows, dh), BF),
            vmem((dh, blocks * 2 * rows), BF),
            vmem((blocks, rows, width), BF),
            vmem((blocks, heads, rows, width), BF),
            vmem((blocks, heads, rows, width), BF),
            vmem((blocks, heads, rows, width), BF),
            vmem((heads, 2, dh, rows), BF),
            vmem((seqs, 2, dh, rows), BF),
            vmem((dh, fh), F32),
            vmem((dh, fh), F32),
            vmem((fh, dh), F32),
            vmem((blocks, rows, width), BF),
            vmem((width, rows), F32),
            vmem((blocks, rows, width), BF),
            vmem((dh, fh), BF),
            vmem((dh, fh), BF),
            vmem((fh, dh), BF),
            vmem((width, depth), BF),
            dma((4,)),
            dma((4,)),
            dma((heads,)),
            dma((heads,)),
            dma((heads,)),
            dma((heads,)),
            dma((heads,)),
            dma((blocks,)),
            dma((blocks,)),
            dma((3,)),
            dma((3,)),
            dma((blocks, heads)),
            dma((blocks, heads)),
            dma((blocks, heads)),
            dma((blocks, heads)),
            dma((seqs, 2)),
            dma((seqs, 2)),
            dma((15 + blocks,)),
        ],
        compiler_params=pltpu.CompilerParams(
            collective_id=0, has_side_effects=True, vmem_limit_bytes=60 * 2**20
        ),
        cost_estimate=pl.CostEstimate(
            flops=5 * 10**9, bytes_accessed=10 * 2**20, transcendentals=2 * 10**6
        ),
        name="layer",
    )(
        queries,
        key_vectors,
        value_vectors,
        jnp.swapaxes(token_rates, 2, 3),
        fast_in,
        fast_gate,
        fast_out,
        out_gain.reshape(1, width),
        out_weight,
        cotangent,
    )
    return pl.pallas_call(
        write_kernel,
        out_shape=shapes,
        in_specs=[hbm] * 5,
        out_specs=(hbm,) * 5,
        scratch_shapes=[vmem(shape.shape, shape.dtype) for shape in shapes] + [dma((2, 10))],
        compiler_params=pltpu.CompilerParams(vmem_limit_bytes=60 * 2**20),
        name="write",
    )(*results)


def pick(mesh):
    fits = mesh.shape["ctx"] == 2 and mesh.shape["seq"] == mesh.shape["head"]

    def body(*args):
        local_heads, dh, _ = args[4].shape
        _, _, rows, width = args[0].shape
        square = dh == rows and width == 2 * rows and local_heads == 2 and args[0].shape[1] == 2
        return (fused_shards if fits and square else shards)(*args)

    return body


def solution(mesh):
    return jax.shard_map(
        pick(mesh),
        mesh=mesh,
        in_specs=(
            P("seq", None, "ctx", "head"),
            P("seq", None, "ctx", "head"),
            P("seq", None, "ctx", "head"),
            P("seq", None, "ctx", "head"),
            P("head", None, None),
            P("head", None, None),
            P("head", None, None),
            P("head"),
            P("head", None),
            P("seq", None, "ctx", "head"),
        ),
        out_specs=(
            P("seq", None, "ctx", "head"),
            P("head", ("seq", "ctx")),
            P("seq", "head", None, None),
            P("seq", "head", None, None),
            P("seq", "head", None, None),
        ),
        check_vma=False,
    )
```

```python
import functools
import math

import jax
import jax.numpy as jnp
from jax import lax
from jax.experimental import pallas as pl
from jax.experimental.pallas import tpu as pltpu
from jax.sharding import PartitionSpec as P


def passed_along(value, axis, steps):
    count = lax.axis_size(axis)
    pairs = [(source, (source + steps) % count) for source in range(count)]
    return lax.ppermute(value, axis, pairs)


def normalize_rms(values_in, epsilon):
    return values_in * lax.rsqrt(jnp.mean(values_in * values_in, axis=-1, keepdims=True) + epsilon)


def column_norms(weight):
    return jnp.sqrt(jnp.sum(weight * weight, axis=-2, keepdims=True) + 1e-06)


def renorm(weight, target):
    return weight * (target / jnp.sqrt(jnp.sum(weight * weight, axis=-2, keepdims=True) + 1e-06))


def shards(
    queries,
    key_vectors,
    value_vectors,
    token_rates,
    fast_in,
    fast_gate,
    fast_out,
    out_gain,
    out_weight,
    cotangent,
):
    local_heads, head_width, hidden_width = fast_in.shape
    block_count = queries.shape[1]
    row_count = queries.shape[2]
    ctx_index = lax.axis_index("ctx")
    query_rows = queries[0].reshape(block_count, row_count, local_heads, head_width)
    key_rows = key_vectors[0].reshape(block_count, row_count, local_heads, head_width)
    value_rows = value_vectors[0].reshape(block_count, row_count, local_heads, head_width)
    weight_in = fast_in.astype(jnp.float32)
    weight_gate = fast_gate.astype(jnp.float32)
    weight_out = fast_out.astype(jnp.float32)
    target_in = column_norms(weight_in)
    target_gate = column_norms(weight_gate)
    target_out = column_norms(weight_out)
    fast_outputs = []
    for block_index in range(block_count):
        query_norm = normalize_rms(query_rows[block_index].astype(jnp.float32), 1e-05).astype(
            jnp.bfloat16
        )
        key_norm = normalize_rms(key_rows[block_index].astype(jnp.float32), 1e-05).astype(
            jnp.bfloat16
        )
        round_in = weight_in.astype(jnp.bfloat16)
        round_gate = weight_gate.astype(jnp.bfloat16)
        round_out = weight_out.astype(jnp.bfloat16)
        hidden = (
            jax.nn.silu(
                jnp.einsum("thd,hdf->thf", query_norm, round_in, preferred_element_type=jnp.float32)
            )
            * jnp.einsum("thd,hdf->thf", query_norm, round_gate, preferred_element_type=jnp.float32)
        ).astype(jnp.bfloat16)
        fast_outputs.append(
            jnp.einsum("thf,hfd->thd", hidden, round_out, preferred_element_type=jnp.float32)
        )
        key_in = jnp.einsum("thd,hdf->thf", key_norm, round_in, preferred_element_type=jnp.float32)
        key_gate = jnp.einsum(
            "thd,hdf->thf", key_norm, round_gate, preferred_element_type=jnp.float32
        )
        sigmoid_in = jax.nn.sigmoid(key_in)
        active = key_in * sigmoid_in
        feature = (active * key_gate).astype(jnp.bfloat16)
        scaled_values = (
            token_rates[0, block_index][:, :, None] * value_rows[block_index].astype(jnp.float32)
        ).astype(jnp.bfloat16)
        d_feature = jnp.einsum(
            "thd,hfd->thf", scaled_values, round_out, preferred_element_type=jnp.float32
        )
        d_in = (d_feature * key_gate * sigmoid_in * (1.0 + key_in * (1.0 - sigmoid_in))).astype(
            jnp.bfloat16
        )
        d_gate = (d_feature * active).astype(jnp.bfloat16)
        update_in = jnp.einsum("thd,thf->hdf", key_norm, d_in, preferred_element_type=jnp.float32)
        update_gate = jnp.einsum(
            "thd,thf->hdf", key_norm, d_gate, preferred_element_type=jnp.float32
        )
        update_out = jnp.einsum(
            "thf,thd->hfd", feature, scaled_values, preferred_element_type=jnp.float32
        )
        total_in, total_gate, total_out = lax.psum((update_in, update_gate, update_out), "ctx")
        weight_in = renorm(weight_in + total_in, target_in)
        weight_gate = renorm(weight_gate + total_gate, target_gate)
        weight_out = renorm(weight_out + total_out, target_out)
    rim_keys, rim_values = passed_along((key_vectors[0], value_vectors[0]), "ctx", 1)
    earlier_keys = jnp.concatenate([jnp.zeros_like(rim_keys[:1]), rim_keys[:-1]], axis=0)
    earlier_values = jnp.concatenate([jnp.zeros_like(rim_values[:1]), rim_values[:-1]], axis=0)
    is_first = ctx_index == 0
    rim_keys = jnp.where(is_first, earlier_keys, rim_keys)
    rim_values = jnp.where(is_first, earlier_values, rim_values)
    window_keys = jnp.concatenate([rim_keys, key_vectors[0]], axis=1).reshape(
        block_count, 2 * row_count, local_heads, head_width
    )
    window_values = jnp.concatenate([rim_values, value_vectors[0]], axis=1).reshape(
        block_count, 2 * row_count, local_heads, head_width
    )
    scores = jnp.einsum(
        "cqhd,ckhd->chqk", query_rows, window_keys, preferred_element_type=jnp.float32
    ) * (1.0 / math.sqrt(head_width))
    query_pos = jnp.arange(row_count, dtype=jnp.int32)[:, None]
    key_pos = jnp.arange(2 * row_count, dtype=jnp.int32)[None, :]
    inside = (key_pos > query_pos) & (key_pos <= query_pos + row_count)
    block_ids = jnp.arange(block_count, dtype=jnp.int32)
    rim_open = (block_ids > 0) | (ctx_index != 0)
    allowed = inside[None, None] & (
        rim_open[:, None, None, None] | (key_pos >= row_count)[None, None]
    )
    scores = jnp.where(allowed, scores, -jnp.inf)
    largest = jnp.max(scores, axis=-1, keepdims=True)
    powers = jnp.exp(scores - largest)
    attn_weights = (powers / jnp.sum(powers, axis=-1, keepdims=True)).astype(jnp.bfloat16)
    attended = jnp.einsum(
        "chqk,ckhd->cqhd", attn_weights, window_values, preferred_element_type=jnp.float32
    )
    fast_stack = jnp.stack(fast_outputs)
    combined = (
        normalize_rms(fast_stack, 1e-05) * out_gain.reshape(local_heads, head_width) + attended
    ).astype(jnp.bfloat16)
    flat_rows = combined.reshape(block_count * row_count, local_heads * head_width)
    partial_out = jnp.dot(flat_rows, out_weight, preferred_element_type=jnp.float32)
    mixed_share = lax.psum_scatter(
        partial_out.astype(jnp.bfloat16), "head", scatter_dimension=1, tiled=True
    )
    layer_out = mixed_share.reshape(1, block_count, row_count, -1)
    piece = lax.all_gather(cotangent, "head", axis=3, tiled=True)
    grad_rows = jnp.einsum(
        "ti,tj->ij",
        flat_rows,
        piece.reshape(-1, piece.shape[3]),
        preferred_element_type=jnp.float32,
    )
    weight_grad = lax.psum_scatter(
        grad_rows.astype(jnp.bfloat16), ("seq", "ctx"), scatter_dimension=1, tiled=True
    ).astype(jnp.float32)
    return (layer_out, weight_grad, weight_in[None], weight_gate[None], weight_out[None])

BF = jnp.bfloat16
F32 = jnp.float32


def mm(left, right):
    return jnp.dot(left, right, preferred_element_type=F32)


def mm_tn(left, right):
    return lax.dot_general(left, right, (((0,), (0,)), ((), ())), preferred_element_type=F32)


def mm_nt(left, right):
    return lax.dot_general(left, right, (((1,), (1,)), ((), ())), preferred_element_type=F32)


def layer_kernel(
    seqs,
    heads,
    q_ref,
    k_ref,
    v_ref,
    rate_ref,
    win_ref,
    wgate_ref,
    wout_ref,
    gain_ref,
    ow_ref,
    cot_ref,
    out_ref,
    grad_ref,
    fin_ref,
    fgate_ref,
    fout_ref,
    qh,
    kh,
    vh,
    svh,
    sv_all,
    cot_all,
    rin,
    rgate,
    rout,
    acc_in,
    acc_gate,
    acc_out,
    fast,
    comb,
    comb_t,
    own,
    part,
    up_buf,
    down_buf,
    gsend,
    grecv,
    last_in,
    last_gate,
    last_out,
    layer,
    grad,
    v_own,
    weights_in,
    weights_gate,
    weights_out,
    ow_own,
    core_s,
    core_r,
    cot_core_s,
    cot_core_r,
    ag_up_s,
    ag_down_s,
    ag_r,
    comb_s,
    comb_r,
    fin_s,
    fin_r,
    up_s,
    up_r,
    down_s,
    down_r,
    g_s,
    g_r,
    local_s,
):
    s = lax.axis_index("seq")
    c = lax.axis_index("ctx")
    h = lax.axis_index("head")
    o = 1 - c
    blocks, rows = q_ref.shape[1], q_ref.shape[2]
    dh = win_ref.shape[1]
    mine = pl.ds(pl.multiple_of(c * dh, dh), dh)
    theirs = pl.ds(pl.multiple_of(o * dh, dh), dh)
    last = heads - 1

    def remote(src, dst, send, recv, where):
        return pltpu.make_async_remote_copy(
            src_ref=src,
            dst_ref=dst,
            send_sem=send,
            recv_sem=recv,
            device_id=where,
            device_id_type=pl.DeviceIdType.MESH,
        )

    fetches = [
        pltpu.make_async_copy(src, dst, local_s.at[n])
        for n, (src, dst) in enumerate(
            (
                (v_ref.at[0], v_own),
                (win_ref.at[c], weights_in),
                (wgate_ref.at[c], weights_gate),
                (wout_ref.at[c], weights_out),
                (ow_ref, ow_own),
            ),
            5,
        )
    ]
    for copy in fetches:
        copy.start()
    fetch_v, *fetch_weights, fetch_ow = fetches

    barrier = pltpu.get_barrier_semaphore()
    for s2 in range(seqs):
        for c2 in range(2):

            @pl.when((s2 != s) | (c2 != c))
            def _():
                pl.semaphore_signal(
                    barrier,
                    inc=1,
                    device_id={"seq": s2, "ctx": c2},
                    device_id_type=pl.DeviceIdType.MESH,
                )

    @pl.when(h < last)
    def _():
        pl.semaphore_signal(
            barrier, inc=1, device_id={"head": h + 1}, device_id_type=pl.DeviceIdType.MESH
        )

    @pl.when(h > 0)
    def _():
        pl.semaphore_signal(
            barrier, inc=1, device_id={"head": h - 1}, device_id_type=pl.DeviceIdType.MESH
        )

    ends = (h == 0).astype(jnp.int32) + (h == last).astype(jnp.int32)
    pl.semaphore_wait(barrier, 2 * seqs - 1 + 2 - ends)

    writes = []

    def write(src, dst, index):
        writes.append(pltpu.make_async_copy(src, dst, local_s.at[index]))
        writes[-1].start()

    def cot_up(owner, b, src=None):
        place = cot_all.at[owner, b, c]
        return remote(
            place if src is None else src,
            place,
            ag_up_s.at[owner, b],
            ag_r.at[owner, b],
            {"head": h + 1},
        )

    def cot_down(owner, b, src=None):
        place = cot_all.at[owner, b, c]
        return remote(
            place if src is None else src,
            place,
            ag_down_s.at[owner, b],
            ag_r.at[owner, b],
            {"head": h - 1},
        )

    def cot_core(owner, src):
        return remote(
            src, cot_all.at[owner, :, c], cot_core_s.at[owner], cot_core_r.at[owner], {"ctx": o}
        )

    def exchange(index, src, dst):
        return remote(src, dst, core_s.at[index], core_r.at[index], {"ctx": o})

    swaps = [
        exchange(0, k_ref.at[0, :, :, theirs], kh.at[:, c]),
        exchange(1, sv_all.at[:, :, theirs], svh.at[:, c]),
        exchange(2, q_ref.at[0, :, :, theirs], qh.at[:, c]),
        exchange(3, v_ref.at[0, :, :, theirs], vh.at[:, c]),
    ]
    swaps[0].start()
    swaps[2].start()
    swaps[3].start()

    @pl.when(h < last)
    def _():
        for b in range(blocks):
            cot_up(h, b, cot_ref.at[0, b]).start()

    @pl.when(h > 0)
    def _():
        for b in range(blocks):
            cot_down(h, b, cot_ref.at[0, b]).start()

    fetch_v.wait()
    for b in range(blocks):
        for i in range(2):
            cols = slice(i * dh, (i + 1) * dh)
            rate = jnp.broadcast_to(rate_ref[0, b, i : i + 1, :], (128, rows)).T[:, :1]
            sv_all[b, :, cols] = (rate * v_own[b, :, cols].astype(F32)).astype(BF)
    swaps[1].start()
    cot_core(h, cot_ref.at[0]).start()
    locals_ = [
        pltpu.make_async_copy(k_ref.at[0, :, :, mine], kh.at[:, c], local_s.at[0]),
        pltpu.make_async_copy(sv_all.at[:, :, mine], svh.at[:, c], local_s.at[1]),
        pltpu.make_async_copy(q_ref.at[0, :, :, mine], qh.at[:, c], local_s.at[2]),
        pltpu.make_async_copy(v_ref.at[0, :, :, mine], vh.at[:, c], local_s.at[3]),
        pltpu.make_async_copy(cot_ref.at[0], cot_all.at[h, :, c], local_s.at[4]),
    ]
    for copy in locals_:
        copy.start()

    def squares(weight):
        return jnp.sum(weight * weight, axis=0, keepdims=True) + 1e-06

    targets = []
    for copy in fetch_weights:
        copy.wait()
    for src, kept in ((weights_in, rin), (weights_gate, rgate), (weights_out, rout)):
        kept[...] = src[...]
        targets.append(jnp.sqrt(squares(src[...].astype(F32))))
    for copy in locals_:
        copy.wait()
    for copy in swaps:
        copy.wait()

    def query_block(b):
        @pl.loop(0, 2)
        def _(i):
            query_norm = normalize_rms(qh[b, i].astype(F32), 1e-05).astype(BF)
            first = mm(query_norm, rin[...])
            hidden = (first * jax.nn.sigmoid(first) * mm(query_norm, rgate[...])).astype(BF)
            fast[i] = mm(hidden, rout[...])

    def key_block(b):
        @pl.loop(0, 2)
        def _(i):
            key_norm = normalize_rms(kh[b, i].astype(F32), 1e-05).astype(BF)
            key_in = mm(key_norm, rin[...])
            key_gate = mm(key_norm, rgate[...])
            scaled = svh[b, i]
            d_feature = mm_nt(scaled, rout[...])
            sigma = jax.nn.sigmoid(key_in)
            active = key_in * sigma
            feature = (active * key_gate).astype(BF)
            d_in = (d_feature * key_gate * sigma * (1.0 + key_in * (1.0 - sigma))).astype(BF)
            d_gate = (d_feature * active).astype(BF)
            up_in = mm_tn(key_norm, d_in)
            up_gate = mm_tn(key_norm, d_gate)
            up_out = mm_tn(feature, scaled)

            @pl.when(i == 0)
            def _():
                acc_in[...] = up_in
                acc_gate[...] = up_gate
                acc_out[...] = up_out

            @pl.when(i == 1)
            def _():
                acc_in[...] += up_in
                acc_gate[...] += up_gate
                acc_out[...] += up_out

        for kept, acc, final, target, start in (
            (rin, acc_in, last_in, targets[0], weights_in),
            (rgate, acc_gate, last_gate, targets[1], weights_gate),
            (rout, acc_out, last_out, targets[2], weights_out),
        ):
            weight = (start[...].astype(F32) if b == 0 else final[...]) + acc[...]
            weight = weight * (target / jnp.sqrt(squares(weight)))
            final[...] = weight
            kept[...] = weight.astype(BF)

    row = lax.broadcasted_iota(jnp.int32, (rows, rows), 0)
    col = lax.broadcasted_iota(jnp.int32, (rows, rows), 1)
    scale = 1.0 / math.sqrt(dh)

    def attend(b, i):
        query = qh[b, i]
        now = jnp.where(col <= row, mm_nt(query, kh[b, i]) * scale, -jnp.inf)
        largest = jnp.max(now, axis=-1, keepdims=True)
        if b == 0 and i == 0:
            powers = jnp.exp(now - largest)
            total = jnp.sum(powers, axis=-1, keepdims=True)
            return mm((powers / total).astype(BF), vh[b, i])
        before = (b, 0) if i == 1 else (b - 1, 1)
        old = jnp.where(col > row, mm_nt(query, kh[before]) * scale, -jnp.inf)
        largest = jnp.maximum(largest, jnp.max(old, axis=-1, keepdims=True))
        powers = jnp.exp(now - largest)
        old_powers = jnp.exp(old - largest)
        total = jnp.sum(powers, axis=-1, keepdims=True) + jnp.sum(
            old_powers, axis=-1, keepdims=True
        )
        return mm((powers / total).astype(BF), vh[b, i]) + mm(
            (old_powers / total).astype(BF), vh[before]
        )

    def comb_copy(b):
        return remote(
            comb.at[b, o], own.at[b, :, mine], comb_s.at[b], comb_r.at[b], {"ctx": o}
        )

    def combine(b):
        for i in range(2):
            value = (
                normalize_rms(fast[i], 1e-05) * gain_ref[:, mine] + attend(b, i)
            ).astype(BF)
            comb[b, i] = value
            at = (b * 2 + i) * rows
            comb_t[:, at : at + rows] = value.T
        comb_copy(b).start()
        own[b, :, mine] = comb[b, c]

    width = ow_own.shape[1] // heads

    def up_copy(b, d):
        return remote(
            part.at[b, d], up_buf.at[b, d], up_s.at[b, d], up_r.at[b, d], {"head": h + 1}
        )

    def down_copy(b, d):
        return remote(
            part.at[b, d], down_buf.at[b, d], down_s.at[b, d], down_r.at[b, d], {"head": h - 1}
        )

    def project(b):
        comb_copy(b).wait()
        rows_in = own[b]
        for d in range(heads):
            part[b, d] = mm(rows_in, ow_own[:, d * width : (d + 1) * width]).astype(BF)

    def drain_up():
        for j in range(last):
            for b in range(blocks):

                @pl.when(j <= h)
                def _(j=j, b=b):
                    cot_up(j, b).wait_send()

    def drain_down():
        for j in range(1, heads):
            for b in range(blocks):

                @pl.when(j >= h)
                def _(j=j, b=b):
                    cot_down(j, b).wait_send()

    def release(b):
        @pl.when(h == 0)
        def _():
            if b == 0:
                drain_up()
            for d in range(last, 0, -1):
                if b > 0:
                    up_copy(b - 1, d).wait_send()
                up_copy(b, d).start()

        @pl.when(h == last)
        def _():
            if b == 0:
                drain_down()
            for d in range(last):
                if b > 0:
                    down_copy(b - 1, d).wait_send()
                down_copy(b, d).start()

    def add(b, d, buf):
        part[b, d] = (part[b, d].astype(F32) + buf[b, d].astype(F32)).astype(BF)

    def forward(b):
        for step in range(1, last):
            d = last + h - step

            @pl.when((h > 0) & (d <= last))
            def _(d=d):
                up_copy(b, d).wait_recv()
                add(b, d, up_buf)
                if b == 0:

                    @pl.when(d == last)
                    def _():
                        drain_up()

                up_copy(b, d).start()

            e = step - (last - h)

            @pl.when((h < last) & (e >= 0))
            def _(e=e):
                down_copy(b, e).wait_recv()
                add(b, e, down_buf)
                if b == 0:

                    @pl.when(e == 0)
                    def _():
                        drain_down()

                down_copy(b, e).start()

    def finish(b):
        @pl.when(h > 0)
        def _():
            up_copy(b, h).wait_recv()
            add(b, h, up_buf)

        @pl.when(h < last)
        def _():
            down_copy(b, h).wait_recv()
            add(b, h, down_buf)

        layer[b] = part[b, h]
        write(layer.at[b], out_ref.at[0, b], 13 + b)
        for d in range(heads):

            @pl.when((d > h) & (h > 0 if b < blocks - 1 else h >= 0))
            def _(d=d):
                up_copy(b, d).wait_send()

            @pl.when((d < h) & (h < last if b < blocks - 1 else h <= last))
            def _(d=d):
                down_copy(b, d).wait_send()

    def gather_step(t, b):
        @pl.when(h - t >= 0)
        def _():
            owner = h - t
            cot_up(owner, b).wait_recv()

            @pl.when(h < last)
            def _():
                cot_up(owner, b).start()

            if b == blocks - 1:
                cot_core(owner, cot_all.at[owner, :, c]).start()

        @pl.when(h + t <= last)
        def _():
            owner = h + t
            cot_down(owner, b).wait_recv()

            @pl.when(h > 0)
            def _():
                cot_down(owner, b).start()

            if b == blocks - 1:
                cot_core(owner, cot_all.at[owner, :, c]).start()

    def g_copy(j, c2):
        return remote(
            gsend.at[j, c2],
            grecv.at[s, c],
            g_s.at[j, c2],
            g_r.at[s, c],
            {"seq": j, "ctx": c2},
        )

    def grad_piece(j):
        cot_core(j, cot_all.at[j, :, c]).wait_recv()
        for c2 in range(2):
            block = cot_all[j, :, :, :, c2 * rows : (c2 + 1) * rows].reshape(-1, rows)
            gsend[j, c2] = mm(comb_t[...], block).astype(BF)

            @pl.when((j != s) | (c2 != c))
            def _(c2=c2):
                g_copy(j, c2).start()

            @pl.when((j == s) & (c2 == c))
            def _(c2=c2):
                grecv[s, c] = gsend[s, c2]

    def grad_step(t):
        @pl.when(h - t >= 0)
        def _():
            grad_piece(h - t)

        if t > 0:

            @pl.when(h + t <= last)
            def _():
                grad_piece(h + t)

    results = ((last_in, fin_ref), (last_gate, fgate_ref), (last_out, fout_ref))
    finals = [
        remote(src, dst.at[0, c], fin_s.at[n], fin_r.at[n], {"ctx": o})
        for n, (src, dst) in enumerate(results)
    ]

    query_block(0)
    combine(0)
    gather_step(1, 0)
    fetch_ow.wait()
    project(0)
    key_block(0)
    gather_step(1, 1)
    release(0)
    query_block(1)
    combine(1)
    if last > 2:
        gather_step(2, 0)
    project(1)
    grad_step(0)
    grad_step(1)
    key_block(1)
    for copy in finals:
        copy.start()
    for n, (src, dst) in enumerate(results):
        write(src, dst.at[0, c], 10 + n)
    for t in range(2, last):
        if t > 2:
            gather_step(t, 0)
        gather_step(t, 1)
    forward(0)
    for t in range(2, last):
        grad_step(t)
    release(1)
    forward(1)
    if last > 1:
        gather_step(last, 0)
        gather_step(last, 1)
        grad_step(last)
    for b in range(blocks):
        finish(b)
    for copy in finals:
        copy.wait()
    for s2 in range(seqs):
        for c2 in range(2):

            @pl.when((s2 != s) | (c2 != c))
            def _(s2=s2, c2=c2):
                remote(
                    gsend.at[s2, c2],
                    grecv.at[s2, c2],
                    g_s.at[s2, c2],
                    g_r.at[s2, c2],
                    {"ctx": o},
                ).wait()

    for i in range(2):
        span = pl.ds(i * dh, dh)
        total = grecv[0, i].astype(F32)
        for s2 in range(1, seqs):
            total = total + grecv[s2, i].astype(F32)
        grad[span, :] = total
        write(grad.at[span, :], grad_ref.at[span, :], 13 + blocks + i)
    for j in range(heads):
        piece = cot_all.at[j, :, c]
        cot_core(j, piece).wait_send()

    for copy in writes:
        copy.wait()


def write_kernel(*refs):
    count = len(refs) // 3
    sems = refs[-1]
    reads, writes = [], []
    for src, dst, held in zip(refs[:count], refs[count : 2 * count], refs[2 * count : -1]):
        if len(src.shape) == 2:
            span = src.shape[0] // 2
            parts = [pl.ds(i * span, span) for i in range(2)]
        else:
            parts = [(0, i) for i in range(2)]
        for at in parts:
            n = len(reads)
            reads.append(pltpu.make_async_copy(src.at[at], held.at[at], sems.at[0, n]))
            writes.append(pltpu.make_async_copy(held.at[at], dst.at[at], sems.at[1, n]))
            reads[-1].start()
    for read, write in zip(reads, writes):
        read.wait()
        write.start()
    for write in writes:
        write.wait()


def fused_shards(
    queries,
    key_vectors,
    value_vectors,
    token_rates,
    fast_in,
    fast_gate,
    fast_out,
    out_gain,
    out_weight,
    cotangent,
):
    seqs, heads = lax.axis_size("seq"), lax.axis_size("head")
    local_heads, dh, fh = fast_in.shape
    _, blocks, rows, width = queries.shape
    depth = out_weight.shape[1]
    vmem, dma = pltpu.VMEM, pltpu.SemaphoreType.DMA
    whole = pl.BlockSpec(memory_space=pltpu.VMEM)
    hbm = pl.BlockSpec(memory_space=pl.ANY)
    shapes = (
        jax.ShapeDtypeStruct((1, blocks, rows, width), BF),
        jax.ShapeDtypeStruct((width, rows), F32),
        jax.ShapeDtypeStruct((1, local_heads, dh, fh), F32),
        jax.ShapeDtypeStruct((1, local_heads, dh, fh), F32),
        jax.ShapeDtypeStruct((1, local_heads, fh, dh), F32),
    )
    results = pl.pallas_call(
        functools.partial(layer_kernel, seqs, heads),
        out_shape=shapes,
        in_specs=[hbm, hbm, hbm, whole, hbm, hbm, hbm, whole, hbm, hbm],
        out_specs=(hbm,) * 5,
        scratch_shapes=[
            vmem((blocks, 2, rows, dh), BF),
            vmem((blocks, 2, rows, dh), BF),
            vmem((blocks, 2, rows, dh), BF),
            vmem((blocks, 2, rows, dh), BF),
            vmem((blocks, rows, width), BF),
            vmem((heads, blocks, 2, rows, width), BF),
            vmem((dh, fh), BF),
            vmem((dh, fh), BF),
            vmem((fh, dh), BF),
            vmem((dh, fh), F32),
            vmem((dh, fh), F32),
            vmem((fh, dh), F32),
            vmem((2, rows, dh), F32),
            vmem((blocks, 2, rows, dh), BF),
            vmem((dh, blocks * 2 * rows), BF),
            vmem((blocks, rows, width), BF),
            vmem((blocks, heads, rows, width), BF),
            vmem((blocks, heads, rows, width), BF),
            vmem((blocks, heads, rows, width), BF),
            vmem((heads, 2, dh, rows), BF),
            vmem((seqs, 2, dh, rows), BF),
            vmem((dh, fh), F32),
            vmem((dh, fh), F32),
            vmem((fh, dh), F32),
            vmem((blocks, rows, width), BF),
            vmem((width, rows), F32),
            vmem((blocks, rows, width), BF),
            vmem((dh, fh), BF),
            vmem((dh, fh), BF),
            vmem((fh, dh), BF),
            vmem((width, depth), BF),
            dma((4,)),
            dma((4,)),
            dma((heads,)),
            dma((heads,)),
            dma((heads, blocks)),
            dma((heads, blocks)),
            dma((heads, blocks)),
            dma((blocks,)),
            dma((blocks,)),
            dma((3,)),
            dma((3,)),
            dma((blocks, heads)),
            dma((blocks, heads)),
            dma((blocks, heads)),
            dma((blocks, heads)),
            dma((seqs, 2)),
            dma((seqs, 2)),
            dma((15 + blocks,)),
        ],
        compiler_params=pltpu.CompilerParams(
            collective_id=0, has_side_effects=True, vmem_limit_bytes=60 * 2**20
        ),
        cost_estimate=pl.CostEstimate(
            flops=5 * 10**9, bytes_accessed=10 * 2**20, transcendentals=2 * 10**6
        ),
        name="layer",
    )(
        queries,
        key_vectors,
        value_vectors,
        jnp.swapaxes(token_rates, 2, 3),
        fast_in,
        fast_gate,
        fast_out,
        out_gain.reshape(1, width),
        out_weight,
        cotangent,
    )
    return pl.pallas_call(
        write_kernel,
        out_shape=shapes,
        in_specs=[hbm] * 5,
        out_specs=(hbm,) * 5,
        scratch_shapes=[vmem(shape.shape, shape.dtype) for shape in shapes] + [dma((2, 10))],
        compiler_params=pltpu.CompilerParams(vmem_limit_bytes=60 * 2**20),
        name="write",
    )(*results)


def pick(mesh):
    fits = mesh.shape["ctx"] == 2 and mesh.shape["seq"] == mesh.shape["head"]

    def body(*args):
        local_heads, dh, _ = args[4].shape
        _, _, rows, width = args[0].shape
        square = dh == rows and width == 2 * rows and local_heads == 2 and args[0].shape[1] == 2
        return (fused_shards if fits and square else shards)(*args)

    return body


def solution(mesh):
    return jax.shard_map(
        pick(mesh),
        mesh=mesh,
        in_specs=(
            P("seq", None, "ctx", "head"),
            P("seq", None, "ctx", "head"),
            P("seq", None, "ctx", "head"),
            P("seq", None, "ctx", "head"),
            P("head", None, None),
            P("head", None, None),
            P("head", None, None),
            P("head"),
            P("head", None),
            P("seq", None, "ctx", "head"),
        ),
        out_specs=(
            P("seq", None, "ctx", "head"),
            P("head", ("seq", "ctx")),
            P("seq", "head", None, None),
            P("seq", "head", None, None),
            P("seq", "head", None, None),
        ),
        check_vma=False,
    )
```

```python
import functools
import math

import jax
import jax.numpy as jnp
from jax import lax
from jax.experimental import pallas as pl
from jax.experimental.pallas import tpu as pltpu
from jax.sharding import PartitionSpec as P


def passed_along(value, axis, steps):
    count = lax.axis_size(axis)
    pairs = [(source, (source + steps) % count) for source in range(count)]
    return lax.ppermute(value, axis, pairs)


def normalize_rms(values_in, epsilon):
    return values_in * lax.rsqrt(jnp.mean(values_in * values_in, axis=-1, keepdims=True) + epsilon)


def column_norms(weight):
    return jnp.sqrt(jnp.sum(weight * weight, axis=-2, keepdims=True) + 1e-06)


def renorm(weight, target):
    return weight * (target / jnp.sqrt(jnp.sum(weight * weight, axis=-2, keepdims=True) + 1e-06))


def shards(
    queries,
    key_vectors,
    value_vectors,
    token_rates,
    fast_in,
    fast_gate,
    fast_out,
    out_gain,
    out_weight,
    cotangent,
):
    local_heads, head_width, hidden_width = fast_in.shape
    block_count = queries.shape[1]
    row_count = queries.shape[2]
    ctx_index = lax.axis_index("ctx")
    query_rows = queries[0].reshape(block_count, row_count, local_heads, head_width)
    key_rows = key_vectors[0].reshape(block_count, row_count, local_heads, head_width)
    value_rows = value_vectors[0].reshape(block_count, row_count, local_heads, head_width)
    weight_in = fast_in.astype(jnp.float32)
    weight_gate = fast_gate.astype(jnp.float32)
    weight_out = fast_out.astype(jnp.float32)
    target_in = column_norms(weight_in)
    target_gate = column_norms(weight_gate)
    target_out = column_norms(weight_out)
    fast_outputs = []
    for block_index in range(block_count):
        query_norm = normalize_rms(query_rows[block_index].astype(jnp.float32), 1e-05).astype(
            jnp.bfloat16
        )
        key_norm = normalize_rms(key_rows[block_index].astype(jnp.float32), 1e-05).astype(
            jnp.bfloat16
        )
        round_in = weight_in.astype(jnp.bfloat16)
        round_gate = weight_gate.astype(jnp.bfloat16)
        round_out = weight_out.astype(jnp.bfloat16)
        hidden = (
            jax.nn.silu(
                jnp.einsum("thd,hdf->thf", query_norm, round_in, preferred_element_type=jnp.float32)
            )
            * jnp.einsum("thd,hdf->thf", query_norm, round_gate, preferred_element_type=jnp.float32)
        ).astype(jnp.bfloat16)
        fast_outputs.append(
            jnp.einsum("thf,hfd->thd", hidden, round_out, preferred_element_type=jnp.float32)
        )
        key_in = jnp.einsum("thd,hdf->thf", key_norm, round_in, preferred_element_type=jnp.float32)
        key_gate = jnp.einsum(
            "thd,hdf->thf", key_norm, round_gate, preferred_element_type=jnp.float32
        )
        sigmoid_in = jax.nn.sigmoid(key_in)
        active = key_in * sigmoid_in
        feature = (active * key_gate).astype(jnp.bfloat16)
        scaled_values = (
            token_rates[0, block_index][:, :, None] * value_rows[block_index].astype(jnp.float32)
        ).astype(jnp.bfloat16)
        d_feature = jnp.einsum(
            "thd,hfd->thf", scaled_values, round_out, preferred_element_type=jnp.float32
        )
        d_in = (d_feature * key_gate * sigmoid_in * (1.0 + key_in * (1.0 - sigmoid_in))).astype(
            jnp.bfloat16
        )
        d_gate = (d_feature * active).astype(jnp.bfloat16)
        update_in = jnp.einsum("thd,thf->hdf", key_norm, d_in, preferred_element_type=jnp.float32)
        update_gate = jnp.einsum(
            "thd,thf->hdf", key_norm, d_gate, preferred_element_type=jnp.float32
        )
        update_out = jnp.einsum(
            "thf,thd->hfd", feature, scaled_values, preferred_element_type=jnp.float32
        )
        total_in, total_gate, total_out = lax.psum((update_in, update_gate, update_out), "ctx")
        weight_in = renorm(weight_in + total_in, target_in)
        weight_gate = renorm(weight_gate + total_gate, target_gate)
        weight_out = renorm(weight_out + total_out, target_out)
    rim_keys, rim_values = passed_along((key_vectors[0], value_vectors[0]), "ctx", 1)
    earlier_keys = jnp.concatenate([jnp.zeros_like(rim_keys[:1]), rim_keys[:-1]], axis=0)
    earlier_values = jnp.concatenate([jnp.zeros_like(rim_values[:1]), rim_values[:-1]], axis=0)
    is_first = ctx_index == 0
    rim_keys = jnp.where(is_first, earlier_keys, rim_keys)
    rim_values = jnp.where(is_first, earlier_values, rim_values)
    window_keys = jnp.concatenate([rim_keys, key_vectors[0]], axis=1).reshape(
        block_count, 2 * row_count, local_heads, head_width
    )
    window_values = jnp.concatenate([rim_values, value_vectors[0]], axis=1).reshape(
        block_count, 2 * row_count, local_heads, head_width
    )
    scores = jnp.einsum(
        "cqhd,ckhd->chqk", query_rows, window_keys, preferred_element_type=jnp.float32
    ) * (1.0 / math.sqrt(head_width))
    query_pos = jnp.arange(row_count, dtype=jnp.int32)[:, None]
    key_pos = jnp.arange(2 * row_count, dtype=jnp.int32)[None, :]
    inside = (key_pos > query_pos) & (key_pos <= query_pos + row_count)
    block_ids = jnp.arange(block_count, dtype=jnp.int32)
    rim_open = (block_ids > 0) | (ctx_index != 0)
    allowed = inside[None, None] & (
        rim_open[:, None, None, None] | (key_pos >= row_count)[None, None]
    )
    scores = jnp.where(allowed, scores, -jnp.inf)
    largest = jnp.max(scores, axis=-1, keepdims=True)
    powers = jnp.exp(scores - largest)
    attn_weights = (powers / jnp.sum(powers, axis=-1, keepdims=True)).astype(jnp.bfloat16)
    attended = jnp.einsum(
        "chqk,ckhd->cqhd", attn_weights, window_values, preferred_element_type=jnp.float32
    )
    fast_stack = jnp.stack(fast_outputs)
    combined = (
        normalize_rms(fast_stack, 1e-05) * out_gain.reshape(local_heads, head_width) + attended
    ).astype(jnp.bfloat16)
    flat_rows = combined.reshape(block_count * row_count, local_heads * head_width)
    partial_out = jnp.dot(flat_rows, out_weight, preferred_element_type=jnp.float32)
    mixed_share = lax.psum_scatter(
        partial_out.astype(jnp.bfloat16), "head", scatter_dimension=1, tiled=True
    )
    layer_out = mixed_share.reshape(1, block_count, row_count, -1)
    piece = lax.all_gather(cotangent, "head", axis=3, tiled=True)
    grad_rows = jnp.einsum(
        "ti,tj->ij",
        flat_rows,
        piece.reshape(-1, piece.shape[3]),
        preferred_element_type=jnp.float32,
    )
    weight_grad = lax.psum_scatter(
        grad_rows.astype(jnp.bfloat16), ("seq", "ctx"), scatter_dimension=1, tiled=True
    ).astype(jnp.float32)
    return (layer_out, weight_grad, weight_in[None], weight_gate[None], weight_out[None])

BF = jnp.bfloat16
F32 = jnp.float32


def mm(left, right):
    return jnp.dot(left, right, preferred_element_type=F32)


def mm_tn(left, right):
    return lax.dot_general(left, right, (((0,), (0,)), ((), ())), preferred_element_type=F32)


def mm_nt(left, right):
    return lax.dot_general(left, right, (((1,), (1,)), ((), ())), preferred_element_type=F32)


def layer_kernel(
    seqs,
    heads,
    q_ref,
    k_ref,
    v_ref,
    rate_ref,
    win_ref,
    wgate_ref,
    wout_ref,
    gain_ref,
    ow_ref,
    cot_ref,
    out_ref,
    grad_ref,
    fin_ref,
    fgate_ref,
    fout_ref,
    qh,
    kh,
    vh,
    svh,
    sv_all,
    cot_all,
    rin,
    rgate,
    rout,
    acc_in,
    acc_gate,
    acc_out,
    fast,
    comb,
    comb_t,
    own,
    part,
    up_buf,
    down_buf,
    gsend,
    grecv,
    last_in,
    last_gate,
    last_out,
    layer,
    grad,
    v_own,
    weights_in,
    weights_gate,
    weights_out,
    ow_own,
    core_s,
    core_r,
    cot_core_s,
    cot_core_r,
    ag_up_s,
    ag_down_s,
    ag_r,
    comb_s,
    comb_r,
    fin_s,
    fin_r,
    up_s,
    up_r,
    down_s,
    down_r,
    g_s,
    g_r,
    local_s,
):
    s = lax.axis_index("seq")
    c = lax.axis_index("ctx")
    h = lax.axis_index("head")
    o = 1 - c
    blocks, rows = q_ref.shape[1], q_ref.shape[2]
    dh = win_ref.shape[1]
    mine = pl.ds(pl.multiple_of(c * dh, dh), dh)
    theirs = pl.ds(pl.multiple_of(o * dh, dh), dh)
    last = heads - 1

    def remote(src, dst, send, recv, where):
        return pltpu.make_async_remote_copy(
            src_ref=src,
            dst_ref=dst,
            send_sem=send,
            recv_sem=recv,
            device_id=where,
            device_id_type=pl.DeviceIdType.MESH,
        )

    fetches = [
        pltpu.make_async_copy(src, dst, local_s.at[n])
        for n, (src, dst) in enumerate(
            (
                (v_ref.at[0], v_own),
                (win_ref.at[c], weights_in),
                (wgate_ref.at[c], weights_gate),
                (wout_ref.at[c], weights_out),
                (ow_ref, ow_own),
            ),
            5,
        )
    ]
    for copy in fetches:
        copy.start()
    fetch_v, *fetch_weights, fetch_ow = fetches

    barrier = pltpu.get_barrier_semaphore()
    for s2 in range(seqs):
        for c2 in range(2):

            @pl.when((s2 != s) | (c2 != c))
            def _():
                pl.semaphore_signal(
                    barrier,
                    inc=1,
                    device_id={"seq": s2, "ctx": c2},
                    device_id_type=pl.DeviceIdType.MESH,
                )

    @pl.when(h < last)
    def _():
        pl.semaphore_signal(
            barrier, inc=1, device_id={"head": h + 1}, device_id_type=pl.DeviceIdType.MESH
        )

    @pl.when(h > 0)
    def _():
        pl.semaphore_signal(
            barrier, inc=1, device_id={"head": h - 1}, device_id_type=pl.DeviceIdType.MESH
        )

    ends = (h == 0).astype(jnp.int32) + (h == last).astype(jnp.int32)
    pl.semaphore_wait(barrier, 2 * seqs - 1 + 2 - ends)

    writes = []

    def write(src, dst, index):
        writes.append(pltpu.make_async_copy(src, dst, local_s.at[index]))
        writes[-1].start()

    def cot_up(owner, b, src=None):
        place = cot_all.at[owner, b, c]
        return remote(
            place if src is None else src,
            place,
            ag_up_s.at[owner, b],
            ag_r.at[owner, b],
            {"head": h + 1},
        )

    def cot_down(owner, b, src=None):
        place = cot_all.at[owner, b, c]
        return remote(
            place if src is None else src,
            place,
            ag_down_s.at[owner, b],
            ag_r.at[owner, b],
            {"head": h - 1},
        )

    def cot_core(owner, src):
        return remote(
            src, cot_all.at[owner, :, c], cot_core_s.at[owner], cot_core_r.at[owner], {"ctx": o}
        )

    def exchange(index, src, dst):
        return remote(src, dst, core_s.at[index], core_r.at[index], {"ctx": o})

    swaps = [
        exchange(0, k_ref.at[0, :, :, theirs], kh.at[:, c]),
        exchange(1, sv_all.at[:, :, theirs], svh.at[:, c]),
        exchange(2, q_ref.at[0, :, :, theirs], qh.at[:, c]),
        exchange(3, v_ref.at[0, :, :, theirs], vh.at[:, c]),
    ]
    swaps[0].start()
    swaps[2].start()
    swaps[3].start()

    @pl.when(h < last)
    def _():
        for b in range(blocks):
            cot_up(h, b, cot_ref.at[0, b]).start()

    @pl.when(h > 0)
    def _():
        for b in range(blocks):
            cot_down(h, b, cot_ref.at[0, b]).start()

    fetch_v.wait()
    for b in range(blocks):
        for i in range(2):
            cols = slice(i * dh, (i + 1) * dh)
            rate = jnp.broadcast_to(rate_ref[0, b, i : i + 1, :], (128, rows)).T[:, :1]
            sv_all[b, :, cols] = (rate * v_own[b, :, cols].astype(F32)).astype(BF)
    swaps[1].start()
    cot_core(h, cot_ref.at[0]).start()
    locals_ = [
        pltpu.make_async_copy(k_ref.at[0, :, :, mine], kh.at[:, c], local_s.at[0]),
        pltpu.make_async_copy(sv_all.at[:, :, mine], svh.at[:, c], local_s.at[1]),
        pltpu.make_async_copy(q_ref.at[0, :, :, mine], qh.at[:, c], local_s.at[2]),
        pltpu.make_async_copy(v_ref.at[0, :, :, mine], vh.at[:, c], local_s.at[3]),
        pltpu.make_async_copy(cot_ref.at[0], cot_all.at[h, :, c], local_s.at[4]),
    ]
    for copy in locals_:
        copy.start()

    def squares(weight):
        return jnp.sum(weight * weight, axis=0, keepdims=True) + 1e-06

    targets = []
    for copy in fetch_weights:
        copy.wait()
    for src, kept in ((weights_in, rin), (weights_gate, rgate), (weights_out, rout)):
        kept[...] = src[...]
        targets.append(jnp.sqrt(squares(src[...].astype(F32))))
    for copy in locals_:
        copy.wait()
    for copy in swaps:
        copy.wait()

    def query_block(b):
        @pl.loop(0, 2)
        def _(i):
            query_norm = normalize_rms(qh[b, i].astype(F32), 1e-05).astype(BF)
            first = mm(query_norm, rin[...])
            hidden = (first * jax.nn.sigmoid(first) * mm(query_norm, rgate[...])).astype(BF)
            fast[i] = mm(hidden, rout[...])

    def key_block(b):
        @pl.loop(0, 2)
        def _(i):
            key_norm = normalize_rms(kh[b, i].astype(F32), 1e-05).astype(BF)
            key_in = mm(key_norm, rin[...])
            key_gate = mm(key_norm, rgate[...])
            scaled = svh[b, i]
            d_feature = mm_nt(scaled, rout[...])
            sigma = jax.nn.sigmoid(key_in)
            active = key_in * sigma
            feature = (active * key_gate).astype(BF)
            d_in = (d_feature * key_gate * sigma * (1.0 + key_in * (1.0 - sigma))).astype(BF)
            d_gate = (d_feature * active).astype(BF)
            up_in = mm_tn(key_norm, d_in)
            up_gate = mm_tn(key_norm, d_gate)
            up_out = mm_tn(feature, scaled)

            @pl.when(i == 0)
            def _():
                acc_in[...] = up_in
                acc_gate[...] = up_gate
                acc_out[...] = up_out

            @pl.when(i == 1)
            def _():
                acc_in[...] += up_in
                acc_gate[...] += up_gate
                acc_out[...] += up_out

        for kept, acc, final, target, start in (
            (rin, acc_in, last_in, targets[0], weights_in),
            (rgate, acc_gate, last_gate, targets[1], weights_gate),
            (rout, acc_out, last_out, targets[2], weights_out),
        ):
            weight = (start[...].astype(F32) if b == 0 else final[...]) + acc[...]
            weight = weight * (target / jnp.sqrt(squares(weight)))
            final[...] = weight
            kept[...] = weight.astype(BF)

    row = lax.broadcasted_iota(jnp.int32, (rows, rows), 0)
    col = lax.broadcasted_iota(jnp.int32, (rows, rows), 1)
    scale = 1.0 / math.sqrt(dh)

    def attend(b, i):
        query = qh[b, i]
        now = jnp.where(col <= row, mm_nt(query, kh[b, i]) * scale, -jnp.inf)
        largest = jnp.max(now, axis=-1, keepdims=True)
        if b == 0 and i == 0:
            powers = jnp.exp(now - largest)
            total = jnp.sum(powers, axis=-1, keepdims=True)
            return mm((powers / total).astype(BF), vh[b, i])
        before = (b, 0) if i == 1 else (b - 1, 1)
        old = jnp.where(col > row, mm_nt(query, kh[before]) * scale, -jnp.inf)
        largest = jnp.maximum(largest, jnp.max(old, axis=-1, keepdims=True))
        powers = jnp.exp(now - largest)
        old_powers = jnp.exp(old - largest)
        total = jnp.sum(powers, axis=-1, keepdims=True) + jnp.sum(
            old_powers, axis=-1, keepdims=True
        )
        return mm((powers / total).astype(BF), vh[b, i]) + mm(
            (old_powers / total).astype(BF), vh[before]
        )

    def comb_copy(b):
        return remote(
            comb.at[b, o], own.at[b, :, mine], comb_s.at[b], comb_r.at[b], {"ctx": o}
        )

    def combine(b):
        for i in range(2):
            value = (
                normalize_rms(fast[i], 1e-05) * gain_ref[:, mine] + attend(b, i)
            ).astype(BF)
            comb[b, i] = value
            at = (b * 2 + i) * rows
            comb_t[:, at : at + rows] = value.T
        comb_copy(b).start()
        own[b, :, mine] = comb[b, c]

    width = ow_own.shape[1] // heads

    def up_copy(b, d):
        return remote(
            part.at[b, d], up_buf.at[b, d], up_s.at[b, d], up_r.at[b, d], {"head": h + 1}
        )

    def down_copy(b, d):
        return remote(
            part.at[b, d], down_buf.at[b, d], down_s.at[b, d], down_r.at[b, d], {"head": h - 1}
        )

    def project(b):
        comb_copy(b).wait()
        rows_in = own[b]
        for d in range(heads):
            part[b, d] = mm(rows_in, ow_own[:, d * width : (d + 1) * width]).astype(BF)

    def drain_up():
        for j in range(last):
            for b in range(blocks):

                @pl.when(j <= h)
                def _(j=j, b=b):
                    cot_up(j, b).wait_send()

    def drain_down():
        for j in range(1, heads):
            for b in range(blocks):

                @pl.when(j >= h)
                def _(j=j, b=b):
                    cot_down(j, b).wait_send()

    def release(b):
        @pl.when(h == 0)
        def _():
            if b == 0:
                drain_up()
            for d in range(last, 0, -1):
                up_copy(b, d).start()

        @pl.when(h == last)
        def _():
            if b == 0:
                drain_down()
            for d in range(last):
                down_copy(b, d).start()

    def add(b, d, buf):
        part[b, d] = (part[b, d].astype(F32) + buf[b, d].astype(F32)).astype(BF)

    def forward(b, step):
        d = last + h - step

        @pl.when((h > 0) & (d <= last))
        def _(d=d):
            up_copy(b, d).wait_recv()
            add(b, d, up_buf)
            if b == 0:

                @pl.when(d == last)
                def _():
                    drain_up()

            up_copy(b, d).start()

        e = step - (last - h)

        @pl.when((h < last) & (e >= 0))
        def _(e=e):
            down_copy(b, e).wait_recv()
            add(b, e, down_buf)
            if b == 0:

                @pl.when(e == 0)
                def _():
                    drain_down()

            down_copy(b, e).start()

    def finish(b):
        @pl.when(h > 0)
        def _():
            up_copy(b, h).wait_recv()
            add(b, h, up_buf)

        @pl.when(h < last)
        def _():
            down_copy(b, h).wait_recv()
            add(b, h, down_buf)

        layer[b] = part[b, h]
        write(layer.at[b], out_ref.at[0, b], 13 + b)
        for d in range(heads):

            @pl.when(d > h)
            def _(d=d):
                up_copy(b, d).wait_send()

            @pl.when(d < h)
            def _(d=d):
                down_copy(b, d).wait_send()

    def gather_step(t, b):
        @pl.when(h - t >= 0)
        def _():
            owner = h - t
            cot_up(owner, b).wait_recv()

            @pl.when(h < last)
            def _():
                cot_up(owner, b).start()

            if b == blocks - 1:
                cot_core(owner, cot_all.at[owner, :, c]).start()

        @pl.when(h + t <= last)
        def _():
            owner = h + t
            cot_down(owner, b).wait_recv()

            @pl.when(h > 0)
            def _():
                cot_down(owner, b).start()

            if b == blocks - 1:
                cot_core(owner, cot_all.at[owner, :, c]).start()

    def g_copy(j, c2):
        return remote(
            gsend.at[j, c2],
            grecv.at[s, c],
            g_s.at[j, c2],
            g_r.at[s, c],
            {"seq": j, "ctx": c2},
        )

    def grad_piece(j):
        cot_core(j, cot_all.at[j, :, c]).wait_recv()
        for c2 in range(2):
            block = cot_all[j, :, :, :, c2 * rows : (c2 + 1) * rows].reshape(-1, rows)
            gsend[j, c2] = mm(comb_t[...], block).astype(BF)

            @pl.when((j != s) | (c2 != c))
            def _(c2=c2):
                g_copy(j, c2).start()

            @pl.when((j == s) & (c2 == c))
            def _(c2=c2):
                grecv[s, c] = gsend[s, c2]

    def grad_step(t):
        @pl.when(h - t >= 0)
        def _():
            grad_piece(h - t)

        if t > 0:

            @pl.when(h + t <= last)
            def _():
                grad_piece(h + t)

    results = ((last_in, fin_ref), (last_gate, fgate_ref), (last_out, fout_ref))
    finals = [
        remote(src, dst.at[0, c], fin_s.at[n], fin_r.at[n], {"ctx": o})
        for n, (src, dst) in enumerate(results)
    ]

    query_block(0)
    combine(0)
    gather_step(1, 0)
    fetch_ow.wait()
    project(0)
    gather_step(1, 1)
    release(0)
    key_block(0)
    query_block(1)
    combine(1)
    if last > 2:
        gather_step(2, 0)
    project(1)
    release(1)
    grad_step(0)
    for t in range(2, last):
        if t > 2:
            gather_step(t, 0)
        gather_step(t, 1)
    grad_step(1)
    if last > 1:
        forward(0, 1)
    key_block(1)
    for copy in finals:
        copy.start()
    for n, (src, dst) in enumerate(results):
        write(src, dst.at[0, c], 10 + n)
    for step in range(2, last):
        forward(0, step)
    for t in range(2, last):
        grad_step(t)
    for step in range(1, last):
        forward(1, step)
    if last > 1:
        gather_step(last, 0)
        gather_step(last, 1)
        grad_step(last)
    for b in range(blocks):
        finish(b)
    for copy in finals:
        copy.wait()
    for s2 in range(seqs):
        for c2 in range(2):

            @pl.when((s2 != s) | (c2 != c))
            def _(s2=s2, c2=c2):
                remote(
                    gsend.at[s2, c2],
                    grecv.at[s2, c2],
                    g_s.at[s2, c2],
                    g_r.at[s2, c2],
                    {"ctx": o},
                ).wait()

    for i in range(2):
        span = pl.ds(i * dh, dh)
        total = grecv[0, i].astype(F32)
        for s2 in range(1, seqs):
            total = total + grecv[s2, i].astype(F32)
        grad[span, :] = total
        write(grad.at[span, :], grad_ref.at[span, :], 13 + blocks + i)
    for j in range(heads):
        piece = cot_all.at[j, :, c]
        cot_core(j, piece).wait_send()

    for copy in writes:
        copy.wait()


def write_kernel(*refs):
    count = len(refs) // 3
    sems = refs[-1]
    reads, writes = [], []
    for src, dst, held in zip(refs[:count], refs[count : 2 * count], refs[2 * count : -1]):
        if len(src.shape) == 2:
            span = src.shape[0] // 2
            parts = [pl.ds(i * span, span) for i in range(2)]
        else:
            parts = [(0, i) for i in range(2)]
        for at in parts:
            n = len(reads)
            reads.append(pltpu.make_async_copy(src.at[at], held.at[at], sems.at[0, n]))
            writes.append(pltpu.make_async_copy(held.at[at], dst.at[at], sems.at[1, n]))
            reads[-1].start()
    for read, write in zip(reads, writes):
        read.wait()
        write.start()
    for write in writes:
        write.wait()


def fused_shards(
    queries,
    key_vectors,
    value_vectors,
    token_rates,
    fast_in,
    fast_gate,
    fast_out,
    out_gain,
    out_weight,
    cotangent,
):
    seqs, heads = lax.axis_size("seq"), lax.axis_size("head")
    local_heads, dh, fh = fast_in.shape
    _, blocks, rows, width = queries.shape
    depth = out_weight.shape[1]
    vmem, dma = pltpu.VMEM, pltpu.SemaphoreType.DMA
    whole = pl.BlockSpec(memory_space=pltpu.VMEM)
    hbm = pl.BlockSpec(memory_space=pl.ANY)
    shapes = (
        jax.ShapeDtypeStruct((1, blocks, rows, width), BF),
        jax.ShapeDtypeStruct((width, rows), F32),
        jax.ShapeDtypeStruct((1, local_heads, dh, fh), F32),
        jax.ShapeDtypeStruct((1, local_heads, dh, fh), F32),
        jax.ShapeDtypeStruct((1, local_heads, fh, dh), F32),
    )
    results = pl.pallas_call(
        functools.partial(layer_kernel, seqs, heads),
        out_shape=shapes,
        in_specs=[hbm, hbm, hbm, whole, hbm, hbm, hbm, whole, hbm, hbm],
        out_specs=(hbm,) * 5,
        scratch_shapes=[
            vmem((blocks, 2, rows, dh), BF),
            vmem((blocks, 2, rows, dh), BF),
            vmem((blocks, 2, rows, dh), BF),
            vmem((blocks, 2, rows, dh), BF),
            vmem((blocks, rows, width), BF),
            vmem((heads, blocks, 2, rows, width), BF),
            vmem((dh, fh), BF),
            vmem((dh, fh), BF),
            vmem((fh, dh), BF),
            vmem((dh, fh), F32),
            vmem((dh, fh), F32),
            vmem((fh, dh), F32),
            vmem((2, rows, dh), F32),
            vmem((blocks, 2, rows, dh), BF),
            vmem((dh, blocks * 2 * rows), BF),
            vmem((blocks, rows, width), BF),
            vmem((blocks, heads, rows, width), BF),
            vmem((blocks, heads, rows, width), BF),
            vmem((blocks, heads, rows, width), BF),
            vmem((heads, 2, dh, rows), BF),
            vmem((seqs, 2, dh, rows), BF),
            vmem((dh, fh), F32),
            vmem((dh, fh), F32),
            vmem((fh, dh), F32),
            vmem((blocks, rows, width), BF),
            vmem((width, rows), F32),
            vmem((blocks, rows, width), BF),
            vmem((dh, fh), BF),
            vmem((dh, fh), BF),
            vmem((fh, dh), BF),
            vmem((width, depth), BF),
            dma((4,)),
            dma((4,)),
            dma((heads,)),
            dma((heads,)),
            dma((heads, blocks)),
            dma((heads, blocks)),
            dma((heads, blocks)),
            dma((blocks,)),
            dma((blocks,)),
            dma((3,)),
            dma((3,)),
            dma((blocks, heads)),
            dma((blocks, heads)),
            dma((blocks, heads)),
            dma((blocks, heads)),
            dma((seqs, 2)),
            dma((seqs, 2)),
            dma((15 + blocks,)),
        ],
        compiler_params=pltpu.CompilerParams(
            collective_id=0, has_side_effects=True, vmem_limit_bytes=60 * 2**20
        ),
        cost_estimate=pl.CostEstimate(
            flops=5 * 10**9, bytes_accessed=10 * 2**20, transcendentals=2 * 10**6
        ),
        name="layer",
    )(
        queries,
        key_vectors,
        value_vectors,
        jnp.swapaxes(token_rates, 2, 3),
        fast_in,
        fast_gate,
        fast_out,
        out_gain.reshape(1, width),
        out_weight,
        cotangent,
    )
    return pl.pallas_call(
        write_kernel,
        out_shape=shapes,
        in_specs=[hbm] * 5,
        out_specs=(hbm,) * 5,
        scratch_shapes=[vmem(shape.shape, shape.dtype) for shape in shapes] + [dma((2, 10))],
        compiler_params=pltpu.CompilerParams(vmem_limit_bytes=60 * 2**20),
        name="write",
    )(*results)


def pick(mesh):
    fits = mesh.shape["ctx"] == 2 and mesh.shape["seq"] == mesh.shape["head"]

    def body(*args):
        local_heads, dh, _ = args[4].shape
        _, _, rows, width = args[0].shape
        square = dh == rows and width == 2 * rows and local_heads == 2 and args[0].shape[1] == 2
        return (fused_shards if fits and square else shards)(*args)

    return body


def solution(mesh):
    return jax.shard_map(
        pick(mesh),
        mesh=mesh,
        in_specs=(
            P("seq", None, "ctx", "head"),
            P("seq", None, "ctx", "head"),
            P("seq", None, "ctx", "head"),
            P("seq", None, "ctx", "head"),
            P("head", None, None),
            P("head", None, None),
            P("head", None, None),
            P("head"),
            P("head", None),
            P("seq", None, "ctx", "head"),
        ),
        out_specs=(
            P("seq", None, "ctx", "head"),
            P("head", ("seq", "ctx")),
            P("seq", "head", None, None),
            P("seq", "head", None, None),
            P("seq", "head", None, None),
        ),
        check_vma=False,
    )
```

```python
import functools
import math

import jax
import jax.numpy as jnp
from jax import lax
from jax.experimental import pallas as pl
from jax.experimental.pallas import tpu as pltpu
from jax.sharding import PartitionSpec as P


def passed_along(value, axis, steps):
    count = lax.axis_size(axis)
    pairs = [(source, (source + steps) % count) for source in range(count)]
    return lax.ppermute(value, axis, pairs)


def normalize_rms(values_in, epsilon):
    return values_in * lax.rsqrt(jnp.mean(values_in * values_in, axis=-1, keepdims=True) + epsilon)


def column_norms(weight):
    return jnp.sqrt(jnp.sum(weight * weight, axis=-2, keepdims=True) + 1e-06)


def renorm(weight, target):
    return weight * (target / jnp.sqrt(jnp.sum(weight * weight, axis=-2, keepdims=True) + 1e-06))


def shards(
    queries,
    key_vectors,
    value_vectors,
    token_rates,
    fast_in,
    fast_gate,
    fast_out,
    out_gain,
    out_weight,
    cotangent,
):
    local_heads, head_width, hidden_width = fast_in.shape
    block_count = queries.shape[1]
    row_count = queries.shape[2]
    ctx_index = lax.axis_index("ctx")
    query_rows = queries[0].reshape(block_count, row_count, local_heads, head_width)
    key_rows = key_vectors[0].reshape(block_count, row_count, local_heads, head_width)
    value_rows = value_vectors[0].reshape(block_count, row_count, local_heads, head_width)
    weight_in = fast_in.astype(jnp.float32)
    weight_gate = fast_gate.astype(jnp.float32)
    weight_out = fast_out.astype(jnp.float32)
    target_in = column_norms(weight_in)
    target_gate = column_norms(weight_gate)
    target_out = column_norms(weight_out)
    fast_outputs = []
    for block_index in range(block_count):
        query_norm = normalize_rms(query_rows[block_index].astype(jnp.float32), 1e-05).astype(
            jnp.bfloat16
        )
        key_norm = normalize_rms(key_rows[block_index].astype(jnp.float32), 1e-05).astype(
            jnp.bfloat16
        )
        round_in = weight_in.astype(jnp.bfloat16)
        round_gate = weight_gate.astype(jnp.bfloat16)
        round_out = weight_out.astype(jnp.bfloat16)
        hidden = (
            jax.nn.silu(
                jnp.einsum("thd,hdf->thf", query_norm, round_in, preferred_element_type=jnp.float32)
            )
            * jnp.einsum("thd,hdf->thf", query_norm, round_gate, preferred_element_type=jnp.float32)
        ).astype(jnp.bfloat16)
        fast_outputs.append(
            jnp.einsum("thf,hfd->thd", hidden, round_out, preferred_element_type=jnp.float32)
        )
        key_in = jnp.einsum("thd,hdf->thf", key_norm, round_in, preferred_element_type=jnp.float32)
        key_gate = jnp.einsum(
            "thd,hdf->thf", key_norm, round_gate, preferred_element_type=jnp.float32
        )
        sigmoid_in = jax.nn.sigmoid(key_in)
        active = key_in * sigmoid_in
        feature = (active * key_gate).astype(jnp.bfloat16)
        scaled_values = (
            token_rates[0, block_index][:, :, None] * value_rows[block_index].astype(jnp.float32)
        ).astype(jnp.bfloat16)
        d_feature = jnp.einsum(
            "thd,hfd->thf", scaled_values, round_out, preferred_element_type=jnp.float32
        )
        d_in = (d_feature * key_gate * sigmoid_in * (1.0 + key_in * (1.0 - sigmoid_in))).astype(
            jnp.bfloat16
        )
        d_gate = (d_feature * active).astype(jnp.bfloat16)
        update_in = jnp.einsum("thd,thf->hdf", key_norm, d_in, preferred_element_type=jnp.float32)
        update_gate = jnp.einsum(
            "thd,thf->hdf", key_norm, d_gate, preferred_element_type=jnp.float32
        )
        update_out = jnp.einsum(
            "thf,thd->hfd", feature, scaled_values, preferred_element_type=jnp.float32
        )
        total_in, total_gate, total_out = lax.psum((update_in, update_gate, update_out), "ctx")
        weight_in = renorm(weight_in + total_in, target_in)
        weight_gate = renorm(weight_gate + total_gate, target_gate)
        weight_out = renorm(weight_out + total_out, target_out)
    rim_keys, rim_values = passed_along((key_vectors[0], value_vectors[0]), "ctx", 1)
    earlier_keys = jnp.concatenate([jnp.zeros_like(rim_keys[:1]), rim_keys[:-1]], axis=0)
    earlier_values = jnp.concatenate([jnp.zeros_like(rim_values[:1]), rim_values[:-1]], axis=0)
    is_first = ctx_index == 0
    rim_keys = jnp.where(is_first, earlier_keys, rim_keys)
    rim_values = jnp.where(is_first, earlier_values, rim_values)
    window_keys = jnp.concatenate([rim_keys, key_vectors[0]], axis=1).reshape(
        block_count, 2 * row_count, local_heads, head_width
    )
    window_values = jnp.concatenate([rim_values, value_vectors[0]], axis=1).reshape(
        block_count, 2 * row_count, local_heads, head_width
    )
    scores = jnp.einsum(
        "cqhd,ckhd->chqk", query_rows, window_keys, preferred_element_type=jnp.float32
    ) * (1.0 / math.sqrt(head_width))
    query_pos = jnp.arange(row_count, dtype=jnp.int32)[:, None]
    key_pos = jnp.arange(2 * row_count, dtype=jnp.int32)[None, :]
    inside = (key_pos > query_pos) & (key_pos <= query_pos + row_count)
    block_ids = jnp.arange(block_count, dtype=jnp.int32)
    rim_open = (block_ids > 0) | (ctx_index != 0)
    allowed = inside[None, None] & (
        rim_open[:, None, None, None] | (key_pos >= row_count)[None, None]
    )
    scores = jnp.where(allowed, scores, -jnp.inf)
    largest = jnp.max(scores, axis=-1, keepdims=True)
    powers = jnp.exp(scores - largest)
    attn_weights = (powers / jnp.sum(powers, axis=-1, keepdims=True)).astype(jnp.bfloat16)
    attended = jnp.einsum(
        "chqk,ckhd->cqhd", attn_weights, window_values, preferred_element_type=jnp.float32
    )
    fast_stack = jnp.stack(fast_outputs)
    combined = (
        normalize_rms(fast_stack, 1e-05) * out_gain.reshape(local_heads, head_width) + attended
    ).astype(jnp.bfloat16)
    flat_rows = combined.reshape(block_count * row_count, local_heads * head_width)
    partial_out = jnp.dot(flat_rows, out_weight, preferred_element_type=jnp.float32)
    mixed_share = lax.psum_scatter(
        partial_out.astype(jnp.bfloat16), "head", scatter_dimension=1, tiled=True
    )
    layer_out = mixed_share.reshape(1, block_count, row_count, -1)
    piece = lax.all_gather(cotangent, "head", axis=3, tiled=True)
    grad_rows = jnp.einsum(
        "ti,tj->ij",
        flat_rows,
        piece.reshape(-1, piece.shape[3]),
        preferred_element_type=jnp.float32,
    )
    weight_grad = lax.psum_scatter(
        grad_rows.astype(jnp.bfloat16), ("seq", "ctx"), scatter_dimension=1, tiled=True
    ).astype(jnp.float32)
    return (layer_out, weight_grad, weight_in[None], weight_gate[None], weight_out[None])

BF = jnp.bfloat16
F32 = jnp.float32


def mm(left, right):
    return jnp.dot(left, right, preferred_element_type=F32)


def mm_tn(left, right):
    return lax.dot_general(left, right, (((0,), (0,)), ((), ())), preferred_element_type=F32)


def mm_nt(left, right):
    return lax.dot_general(left, right, (((1,), (1,)), ((), ())), preferred_element_type=F32)


def layer_kernel(
    seqs,
    heads,
    q_ref,
    k_ref,
    v_ref,
    rate_ref,
    win_ref,
    wgate_ref,
    wout_ref,
    gain_ref,
    ow_ref,
    cot_ref,
    out_ref,
    grad_ref,
    fin_ref,
    fgate_ref,
    fout_ref,
    qh,
    kh,
    vh,
    svh,
    sv_all,
    cot_all,
    rin,
    rgate,
    rout,
    acc_in,
    acc_gate,
    acc_out,
    fast,
    comb,
    comb_t,
    own,
    part,
    up_buf,
    down_buf,
    gsend,
    grecv,
    last_in,
    last_gate,
    last_out,
    layer,
    grad,
    v_own,
    weights_in,
    weights_gate,
    weights_out,
    ow_own,
    core_s,
    core_r,
    cot_core_s,
    cot_core_r,
    ag_up_s,
    ag_down_s,
    ag_r,
    comb_s,
    comb_r,
    fin_s,
    fin_r,
    up_s,
    up_r,
    down_s,
    down_r,
    g_s,
    g_r,
    local_s,
):
    s = lax.axis_index("seq")
    c = lax.axis_index("ctx")
    h = lax.axis_index("head")
    o = 1 - c
    blocks, rows = q_ref.shape[1], q_ref.shape[2]
    dh = win_ref.shape[1]
    mine = pl.ds(pl.multiple_of(c * dh, dh), dh)
    theirs = pl.ds(pl.multiple_of(o * dh, dh), dh)
    last = heads - 1

    def remote(src, dst, send, recv, where):
        return pltpu.make_async_remote_copy(
            src_ref=src,
            dst_ref=dst,
            send_sem=send,
            recv_sem=recv,
            device_id=where,
            device_id_type=pl.DeviceIdType.MESH,
        )

    fetches = [
        pltpu.make_async_copy(src, dst, local_s.at[n])
        for n, (src, dst) in enumerate(
            (
                (v_ref.at[0], v_own),
                (win_ref.at[c], weights_in),
                (wgate_ref.at[c], weights_gate),
                (wout_ref.at[c], weights_out),
                (ow_ref, ow_own),
            ),
            5,
        )
    ]
    for copy in fetches:
        copy.start()
    fetch_v, *fetch_weights, fetch_ow = fetches

    barrier = pltpu.get_barrier_semaphore()
    for s2 in range(seqs):
        for c2 in range(2):

            @pl.when((s2 != s) | (c2 != c))
            def _():
                pl.semaphore_signal(
                    barrier,
                    inc=1,
                    device_id={"seq": s2, "ctx": c2},
                    device_id_type=pl.DeviceIdType.MESH,
                )

    @pl.when(h < last)
    def _():
        pl.semaphore_signal(
            barrier, inc=1, device_id={"head": h + 1}, device_id_type=pl.DeviceIdType.MESH
        )

    @pl.when(h > 0)
    def _():
        pl.semaphore_signal(
            barrier, inc=1, device_id={"head": h - 1}, device_id_type=pl.DeviceIdType.MESH
        )

    ends = (h == 0).astype(jnp.int32) + (h == last).astype(jnp.int32)
    pl.semaphore_wait(barrier, 2 * seqs - 1 + 2 - ends)

    writes = []

    def write(src, dst, index):
        writes.append(pltpu.make_async_copy(src, dst, local_s.at[index]))
        writes[-1].start()

    def cot_up(owner, b, src=None):
        place = cot_all.at[owner, b, c]
        return remote(
            place if src is None else src,
            place,
            ag_up_s.at[owner, b],
            ag_r.at[owner, b],
            {"head": h + 1},
        )

    def cot_down(owner, b, src=None):
        place = cot_all.at[owner, b, c]
        return remote(
            place if src is None else src,
            place,
            ag_down_s.at[owner, b],
            ag_r.at[owner, b],
            {"head": h - 1},
        )

    def cot_core(owner, src):
        return remote(
            src, cot_all.at[owner, :, c], cot_core_s.at[owner], cot_core_r.at[owner], {"ctx": o}
        )

    def exchange(index, src, dst):
        return remote(src, dst, core_s.at[index], core_r.at[index], {"ctx": o})

    swaps = [
        exchange(0, k_ref.at[0, :, :, theirs], kh.at[:, c]),
        exchange(1, sv_all.at[:, :, theirs], svh.at[:, c]),
        exchange(2, q_ref.at[0, :, :, theirs], qh.at[:, c]),
        exchange(3, v_ref.at[0, :, :, theirs], vh.at[:, c]),
    ]
    swaps[0].start()
    swaps[2].start()
    swaps[3].start()

    @pl.when(h < last)
    def _():
        for b in range(blocks):
            cot_up(h, b, cot_ref.at[0, b]).start()

    @pl.when(h > 0)
    def _():
        for b in range(blocks):
            cot_down(h, b, cot_ref.at[0, b]).start()

    fetch_v.wait()
    for b in range(blocks):
        for i in range(2):
            cols = slice(i * dh, (i + 1) * dh)
            rate = jnp.broadcast_to(rate_ref[0, b, i : i + 1, :], (128, rows)).T[:, :1]
            sv_all[b, :, cols] = (rate * v_own[b, :, cols].astype(F32)).astype(BF)
    swaps[1].start()
    cot_core(h, cot_ref.at[0]).start()
    locals_ = [
        pltpu.make_async_copy(k_ref.at[0, :, :, mine], kh.at[:, c], local_s.at[0]),
        pltpu.make_async_copy(sv_all.at[:, :, mine], svh.at[:, c], local_s.at[1]),
        pltpu.make_async_copy(q_ref.at[0, :, :, mine], qh.at[:, c], local_s.at[2]),
        pltpu.make_async_copy(v_ref.at[0, :, :, mine], vh.at[:, c], local_s.at[3]),
        pltpu.make_async_copy(cot_ref.at[0], cot_all.at[h, :, c], local_s.at[4]),
    ]
    for copy in locals_:
        copy.start()

    def squares(weight):
        return jnp.sum(weight * weight, axis=0, keepdims=True) + 1e-06

    targets = []
    for copy in fetch_weights:
        copy.wait()
    for src, kept in ((weights_in, rin), (weights_gate, rgate), (weights_out, rout)):
        kept[...] = src[...]
        targets.append(jnp.sqrt(squares(src[...].astype(F32))))
    for copy in locals_:
        copy.wait()
    for copy in swaps:
        copy.wait()

    def query_block(b):
        @pl.loop(0, 2)
        def _(i):
            query_norm = normalize_rms(qh[b, i].astype(F32), 1e-05).astype(BF)
            first = mm(query_norm, rin[...])
            hidden = (first * jax.nn.sigmoid(first) * mm(query_norm, rgate[...])).astype(BF)
            fast[i] = mm(hidden, rout[...])

    def key_block(b):
        @pl.loop(0, 2)
        def _(i):
            key_norm = normalize_rms(kh[b, i].astype(F32), 1e-05).astype(BF)
            key_in = mm(key_norm, rin[...])
            key_gate = mm(key_norm, rgate[...])
            scaled = svh[b, i]
            d_feature = mm_nt(scaled, rout[...])
            sigma = jax.nn.sigmoid(key_in)
            active = key_in * sigma
            feature = (active * key_gate).astype(BF)
            d_in = (d_feature * key_gate * sigma * (1.0 + key_in * (1.0 - sigma))).astype(BF)
            d_gate = (d_feature * active).astype(BF)
            up_in = mm_tn(key_norm, d_in)
            up_gate = mm_tn(key_norm, d_gate)
            up_out = mm_tn(feature, scaled)

            @pl.when(i == 0)
            def _():
                acc_in[...] = up_in
                acc_gate[...] = up_gate
                acc_out[...] = up_out

            @pl.when(i == 1)
            def _():
                acc_in[...] += up_in
                acc_gate[...] += up_gate
                acc_out[...] += up_out

        for kept, acc, final, target, start in (
            (rin, acc_in, last_in, targets[0], weights_in),
            (rgate, acc_gate, last_gate, targets[1], weights_gate),
            (rout, acc_out, last_out, targets[2], weights_out),
        ):
            weight = (start[...].astype(F32) if b == 0 else final[...]) + acc[...]
            weight = weight * (target / jnp.sqrt(squares(weight)))
            final[...] = weight
            kept[...] = weight.astype(BF)

    row = lax.broadcasted_iota(jnp.int32, (rows, rows), 0)
    col = lax.broadcasted_iota(jnp.int32, (rows, rows), 1)
    scale = 1.0 / math.sqrt(dh)

    def attend(b, i):
        query = qh[b, i]
        now = jnp.where(col <= row, mm_nt(query, kh[b, i]) * scale, -jnp.inf)
        largest = jnp.max(now, axis=-1, keepdims=True)
        if b == 0 and i == 0:
            powers = jnp.exp(now - largest)
            total = jnp.sum(powers, axis=-1, keepdims=True)
            return mm((powers / total).astype(BF), vh[b, i])
        before = (b, 0) if i == 1 else (b - 1, 1)
        old = jnp.where(col > row, mm_nt(query, kh[before]) * scale, -jnp.inf)
        largest = jnp.maximum(largest, jnp.max(old, axis=-1, keepdims=True))
        powers = jnp.exp(now - largest)
        old_powers = jnp.exp(old - largest)
        total = jnp.sum(powers, axis=-1, keepdims=True) + jnp.sum(
            old_powers, axis=-1, keepdims=True
        )
        return mm((powers / total).astype(BF), vh[b, i]) + mm(
            (old_powers / total).astype(BF), vh[before]
        )

    def comb_copy(b):
        return remote(
            comb.at[b, o], own.at[b, :, mine], comb_s.at[b], comb_r.at[b], {"ctx": o}
        )

    def combine(b):
        for i in range(2):
            value = (
                normalize_rms(fast[i], 1e-05) * gain_ref[:, mine] + attend(b, i)
            ).astype(BF)
            comb[b, i] = value
            at = (b * 2 + i) * rows
            comb_t[:, at : at + rows] = value.T
        comb_copy(b).start()
        own[b, :, mine] = comb[b, c]

    width = ow_own.shape[1] // heads

    def up_copy(b, d):
        return remote(
            part.at[b, d], up_buf.at[b, d], up_s.at[b, d], up_r.at[b, d], {"head": h + 1}
        )

    def down_copy(b, d):
        return remote(
            part.at[b, d], down_buf.at[b, d], down_s.at[b, d], down_r.at[b, d], {"head": h - 1}
        )

    def project(b):
        comb_copy(b).wait()
        rows_in = own[b]
        for d in range(heads):
            part[b, d] = mm(rows_in, ow_own[:, d * width : (d + 1) * width]).astype(BF)

    def drain_up():
        for j in range(last):
            for b in range(blocks):

                @pl.when(j <= h)
                def _(j=j, b=b):
                    cot_up(j, b).wait_send()

    def drain_down():
        for j in range(1, heads):
            for b in range(blocks):

                @pl.when(j >= h)
                def _(j=j, b=b):
                    cot_down(j, b).wait_send()

    def release(b):
        @pl.when(h == 0)
        def _():
            if b == 0:
                drain_up()
            for d in range(last, 0, -1):
                if b > 0:
                    up_copy(b - 1, d).wait_send()
                up_copy(b, d).start()

        @pl.when(h == last)
        def _():
            if b == 0:
                drain_down()
            for d in range(last):
                if b > 0:
                    down_copy(b - 1, d).wait_send()
                down_copy(b, d).start()

    def add(b, d, buf):
        part[b, d] = (part[b, d].astype(F32) + buf[b, d].astype(F32)).astype(BF)

    def forward(b):
        for step in range(1, last):
            d = last + h - step

            @pl.when((h > 0) & (d <= last))
            def _(d=d):
                up_copy(b, d).wait_recv()
                add(b, d, up_buf)
                if b == 0:

                    @pl.when(d == last)
                    def _():
                        drain_up()

                up_copy(b, d).start()

            e = step - (last - h)

            @pl.when((h < last) & (e >= 0))
            def _(e=e):
                down_copy(b, e).wait_recv()
                add(b, e, down_buf)
                if b == 0:

                    @pl.when(e == 0)
                    def _():
                        drain_down()

                down_copy(b, e).start()

    def finish(b):
        @pl.when(h > 0)
        def _():
            up_copy(b, h).wait_recv()
            add(b, h, up_buf)

        @pl.when(h < last)
        def _():
            down_copy(b, h).wait_recv()
            add(b, h, down_buf)

        layer[b] = part[b, h]
        write(layer.at[b], out_ref.at[0, b], 13 + b)
        for d in range(heads):

            @pl.when((d > h) & (h > 0 if b < blocks - 1 else h >= 0))
            def _(d=d):
                up_copy(b, d).wait_send()

            @pl.when((d < h) & (h < last if b < blocks - 1 else h <= last))
            def _(d=d):
                down_copy(b, d).wait_send()

    def gather_step(t, b):
        @pl.when(h - t >= 0)
        def _():
            owner = h - t
            cot_up(owner, b).wait_recv()

            @pl.when(h < last)
            def _():
                cot_up(owner, b).start()

            if b == blocks - 1:
                cot_core(owner, cot_all.at[owner, :, c]).start()

        @pl.when(h + t <= last)
        def _():
            owner = h + t
            cot_down(owner, b).wait_recv()

            @pl.when(h > 0)
            def _():
                cot_down(owner, b).start()

            if b == blocks - 1:
                cot_core(owner, cot_all.at[owner, :, c]).start()

    def g_copy(j, c2):
        return remote(
            gsend.at[j, c2],
            grecv.at[s, c],
            g_s.at[j, c2],
            g_r.at[s, c],
            {"seq": j, "ctx": c2},
        )

    def grad_piece(j):
        cot_core(j, cot_all.at[j, :, c]).wait_recv()
        for c2 in range(2):
            block = cot_all[j, :, :, :, c2 * rows : (c2 + 1) * rows].reshape(-1, rows)
            gsend[j, c2] = mm(comb_t[...], block).astype(BF)

            @pl.when((j != s) | (c2 != c))
            def _(c2=c2):
                g_copy(j, c2).start()

            @pl.when((j == s) & (c2 == c))
            def _(c2=c2):
                grecv[s, c] = gsend[s, c2]

    def grad_step(t):
        @pl.when(h - t >= 0)
        def _():
            grad_piece(h - t)

        if t > 0:

            @pl.when(h + t <= last)
            def _():
                grad_piece(h + t)

    results = ((last_in, fin_ref), (last_gate, fgate_ref), (last_out, fout_ref))
    finals = [
        remote(src, dst.at[0, c], fin_s.at[n], fin_r.at[n], {"ctx": o})
        for n, (src, dst) in enumerate(results)
    ]

    query_block(0)
    combine(0)
    gather_step(1, 0)
    fetch_ow.wait()
    project(0)
    key_block(0)
    gather_step(1, 1)
    release(0)
    query_block(1)
    combine(1)
    if last > 2:
        gather_step(2, 0)
    project(1)
    grad_step(0)
    grad_step(1)
    key_block(1)
    for copy in finals:
        copy.start()
    for n, (src, dst) in enumerate(results):
        write(src, dst.at[0, c], 10 + n)
    for t in range(2, last):
        if t > 2:
            gather_step(t, 0)
        gather_step(t, 1)
    forward(0)
    for t in range(2, last):
        grad_step(t)
    release(1)
    forward(1)
    for b in range(blocks - 1):
        finish(b)
    if last > 1:
        gather_step(last, 0)
        gather_step(last, 1)
        grad_step(last)
    finish(blocks - 1)
    for copy in finals:
        copy.wait()
    for s2 in range(seqs):
        for c2 in range(2):

            @pl.when((s2 != s) | (c2 != c))
            def _(s2=s2, c2=c2):
                remote(
                    gsend.at[s2, c2],
                    grecv.at[s2, c2],
                    g_s.at[s2, c2],
                    g_r.at[s2, c2],
                    {"ctx": o},
                ).wait()

    for i in range(2):
        span = pl.ds(i * dh, dh)
        total = grecv[0, i].astype(F32)
        for s2 in range(1, seqs):
            total = total + grecv[s2, i].astype(F32)
        grad[span, :] = total
        write(grad.at[span, :], grad_ref.at[span, :], 13 + blocks + i)
    for j in range(heads):
        piece = cot_all.at[j, :, c]
        cot_core(j, piece).wait_send()

    for copy in writes:
        copy.wait()


def write_kernel(*refs):
    count = len(refs) // 3
    sems = refs[-1]
    reads, writes = [], []
    for src, dst, held in zip(refs[:count], refs[count : 2 * count], refs[2 * count : -1]):
        if len(src.shape) == 2:
            span = src.shape[0] // 2
            parts = [pl.ds(i * span, span) for i in range(2)]
        else:
            parts = [(0, i) for i in range(2)]
        for at in parts:
            n = len(reads)
            reads.append(pltpu.make_async_copy(src.at[at], held.at[at], sems.at[0, n]))
            writes.append(pltpu.make_async_copy(held.at[at], dst.at[at], sems.at[1, n]))
            reads[-1].start()
    for read, write in zip(reads, writes):
        read.wait()
        write.start()
    for write in writes:
        write.wait()


def fused_shards(
    queries,
    key_vectors,
    value_vectors,
    token_rates,
    fast_in,
    fast_gate,
    fast_out,
    out_gain,
    out_weight,
    cotangent,
):
    seqs, heads = lax.axis_size("seq"), lax.axis_size("head")
    local_heads, dh, fh = fast_in.shape
    _, blocks, rows, width = queries.shape
    depth = out_weight.shape[1]
    vmem, dma = pltpu.VMEM, pltpu.SemaphoreType.DMA
    whole = pl.BlockSpec(memory_space=pltpu.VMEM)
    hbm = pl.BlockSpec(memory_space=pl.ANY)
    shapes = (
        jax.ShapeDtypeStruct((1, blocks, rows, width), BF),
        jax.ShapeDtypeStruct((width, rows), F32),
        jax.ShapeDtypeStruct((1, local_heads, dh, fh), F32),
        jax.ShapeDtypeStruct((1, local_heads, dh, fh), F32),
        jax.ShapeDtypeStruct((1, local_heads, fh, dh), F32),
    )
    results = pl.pallas_call(
        functools.partial(layer_kernel, seqs, heads),
        out_shape=shapes,
        in_specs=[hbm, hbm, hbm, whole, hbm, hbm, hbm, whole, hbm, hbm],
        out_specs=(hbm,) * 5,
        scratch_shapes=[
            vmem((blocks, 2, rows, dh), BF),
            vmem((blocks, 2, rows, dh), BF),
            vmem((blocks, 2, rows, dh), BF),
            vmem((blocks, 2, rows, dh), BF),
            vmem((blocks, rows, width), BF),
            vmem((heads, blocks, 2, rows, width), BF),
            vmem((dh, fh), BF),
            vmem((dh, fh), BF),
            vmem((fh, dh), BF),
            vmem((dh, fh), F32),
            vmem((dh, fh), F32),
            vmem((fh, dh), F32),
            vmem((2, rows, dh), F32),
            vmem((blocks, 2, rows, dh), BF),
            vmem((dh, blocks * 2 * rows), BF),
            vmem((blocks, rows, width), BF),
            vmem((blocks, heads, rows, width), BF),
            vmem((blocks, heads, rows, width), BF),
            vmem((blocks, heads, rows, width), BF),
            vmem((heads, 2, dh, rows), BF),
            vmem((seqs, 2, dh, rows), BF),
            vmem((dh, fh), F32),
            vmem((dh, fh), F32),
            vmem((fh, dh), F32),
            vmem((blocks, rows, width), BF),
            vmem((width, rows), F32),
            vmem((blocks, rows, width), BF),
            vmem((dh, fh), BF),
            vmem((dh, fh), BF),
            vmem((fh, dh), BF),
            vmem((width, depth), BF),
            dma((4,)),
            dma((4,)),
            dma((heads,)),
            dma((heads,)),
            dma((heads, blocks)),
            dma((heads, blocks)),
            dma((heads, blocks)),
            dma((blocks,)),
            dma((blocks,)),
            dma((3,)),
            dma((3,)),
            dma((blocks, heads)),
            dma((blocks, heads)),
            dma((blocks, heads)),
            dma((blocks, heads)),
            dma((seqs, 2)),
            dma((seqs, 2)),
            dma((15 + blocks,)),
        ],
        compiler_params=pltpu.CompilerParams(
            collective_id=0, has_side_effects=True, vmem_limit_bytes=60 * 2**20
        ),
        cost_estimate=pl.CostEstimate(
            flops=5 * 10**9, bytes_accessed=10 * 2**20, transcendentals=2 * 10**6
        ),
        name="layer",
    )(
        queries,
        key_vectors,
        value_vectors,
        jnp.swapaxes(token_rates, 2, 3),
        fast_in,
        fast_gate,
        fast_out,
        out_gain.reshape(1, width),
        out_weight,
        cotangent,
    )
    return pl.pallas_call(
        write_kernel,
        out_shape=shapes,
        in_specs=[hbm] * 5,
        out_specs=(hbm,) * 5,
        scratch_shapes=[vmem(shape.shape, shape.dtype) for shape in shapes] + [dma((2, 10))],
        compiler_params=pltpu.CompilerParams(vmem_limit_bytes=60 * 2**20),
        name="write",
    )(*results)


def pick(mesh):
    fits = mesh.shape["ctx"] == 2 and mesh.shape["seq"] == mesh.shape["head"]

    def body(*args):
        local_heads, dh, _ = args[4].shape
        _, _, rows, width = args[0].shape
        square = dh == rows and width == 2 * rows and local_heads == 2 and args[0].shape[1] == 2
        return (fused_shards if fits and square else shards)(*args)

    return body


def solution(mesh):
    return jax.shard_map(
        pick(mesh),
        mesh=mesh,
        in_specs=(
            P("seq", None, "ctx", "head"),
            P("seq", None, "ctx", "head"),
            P("seq", None, "ctx", "head"),
            P("seq", None, "ctx", "head"),
            P("head", None, None),
            P("head", None, None),
            P("head", None, None),
            P("head"),
            P("head", None),
            P("seq", None, "ctx", "head"),
        ),
        out_specs=(
            P("seq", None, "ctx", "head"),
            P("head", ("seq", "ctx")),
            P("seq", "head", None, None),
            P("seq", "head", None, None),
            P("seq", "head", None, None),
        ),
        check_vma=False,
    )
```
